32 devices in a mesh: sub: 8 (over y, x, core), coarse: 4 (over z).
Axes of the slice: x: 2, y: 2, z: 4, core: 2. Of those that a mesh axis runs over, the one named last changes fastest.
Arguments:
- deflation: float32 [8, 64, 64, 512], P('sub', None, 'coarse')
- conductivity: float32 [8, 64, 512], P('sub', 'coarse'), may hold values from 0.1 to 10
- storage: float32 [8, 64, 512], P('sub', 'coarse'), may hold values from 0.5 to 4
- interface_rows: int32 [8, 4, 8, 512], P('sub', 'coarse'), may hold values from 0 to 8191, as said below
- interface_counts: int32 [8, 4, 8], P('sub', 'coarse'), may hold values from 0 to 512, as said below
Outputs:
- coarse_factor: float32 [8, 256, 256], P('sub')
- panel_rows: float32 [8, 4, 256, 512], P('sub', 'coarse')
The draws below stay inside these ranges and needn't reach their ends.
Inputs may be any that keep to these rules, and one draw needn't show every extreme that they name: Slot j of a subdomain names the column offset o = j - 4 for j < 4 and j - 3 otherwise; interface_counts[a, c, slot of o] equals interface_counts[a + o, c, slot of -o], and is 0 where a + o lies outside 0 to 7. The most, 512, is reached in every draw. `interface_rows`: slots j < 4 hold cells with x = 0, the others cells with x = 15. Entries past a slot's count are also such cells and carry no edge.
All inputs are finite; a program needn't handle non-finite values.
Results may differ from the reference program's by a relative error of at most 0.0003.
Values sent between devices are 32-bit elements; how exact they have to be, the bound alone decides.
A program may use at most 64 MiB of HBM per device.

```python
import math
import jax
import jax.numpy as jnp
from jax import lax

K = 64
CX = 16
CY = 32
CZ = 16
PAD = 512
REACH = 4
COLUMNS = 8
NZ = 64
N_SUB = 8
N_COARSE = 4


def draw_deflation(key, part):
    noise_key = jax.random.fold_in(key, 21)
    amplitude_key = jax.random.fold_in(key, 22)
    noise = jax.random.normal(noise_key, (N_SUB, K, NZ, CX * CY), jnp.float32)
    amplitude = 1.5 * jax.random.normal(amplitude_key, (N_SUB, K, NZ, 1), jnp.float32)
    return ((noise + amplitude) / math.sqrt(CX * CY)).astype(jnp.float32)


def draw_interface_rows(key, part):
    row_key = jax.random.fold_in(key, 41)
    layer_key = jax.random.fold_in(key, 42)
    shape = (N_SUB, N_COARSE, 2 * REACH, PAD)
    row_y = jax.random.randint(row_key, shape, 0, CY)
    layer_z = jax.random.randint(layer_key, shape, 0, CZ)
    slot = jnp.arange(2 * REACH)[None, None, :, None]
    edge_x = jnp.where(slot < REACH, 0, CX - 1)
    return (layer_z * (CX * CY) + row_y * CX + edge_x).astype(jnp.int32)


def draw_interface_counts(key, part):
    first_key = jax.random.fold_in(key, 31)
    second_key = jax.random.fold_in(key, 32)
    third_key = jax.random.fold_in(key, 33)
    forward = jax.random.randint(first_key, (N_SUB, N_COARSE, REACH), 1, PAD + 1)
    absent = jax.random.randint(second_key, (N_SUB, N_COARSE, REACH), 0, 4) == 0
    forward = jnp.where(absent, 0, forward)
    chosen = jax.random.randint(third_key, (), 0, N_SUB - 1)
    column = jnp.arange(N_SUB)[:, None, None]
    reach_id = jnp.arange(REACH)[None, None, :]
    forward = jnp.where((column == chosen) & (reach_id == 0), PAD, forward)
    column_two = jnp.arange(N_SUB)[:, None]
    slots = []
    for offset in range(-REACH, 0):
        distance = -offset
        shifted = jnp.roll(forward[:, :, distance - 1], distance, axis=0)
        slots.append(jnp.where(column_two >= distance, shifted, 0))
    for offset in range(1, REACH + 1):
        slots.append(jnp.where(column_two < N_SUB - offset, forward[:, :, offset - 1], 0))
    return jnp.stack(slots, axis=-1).astype(jnp.int32)


def level_of(rng, shape, cuts, smallest, high):
    gain = 1.0
    for dim, shards_of in cuts:
        draws = jax.random.uniform(jax.random.fold_in(jax.random.fold_in(rng, 6), dim), (shards_of,), jnp.float32, smallest / len(cuts), high / len(cuts))
        gain = gain * jnp.repeat(jnp.exp(draws), shape[dim] // shards_of).reshape((-1,) + (1,) * (len(shape) - 1 - dim))
    return gain


def setup_inputs(seed: int = 0) -> dict:
    seeds = jax.random.split(jax.random.key(seed), 6)
    return {
        "deflation": draw_deflation(jax.random.fold_in(seeds[5], 71), 0),
        "conductivity": jnp.clip(jnp.exp(math.log(10.0) - 4.6051702 * jax.random.uniform(seeds[1], (COLUMNS, NZ, CX * CY), jnp.float32) ** level_of(seeds[1], (COLUMNS, NZ, CX * CY), ((0, 8), (1, 4)), -0.2, 0.2)), 0.1, 10.0),
        "storage": jnp.clip(jnp.exp(math.log(4.0) - 2.0794415 * jax.random.uniform(seeds[2], (COLUMNS, NZ, CX * CY), jnp.float32) ** level_of(seeds[2], (COLUMNS, NZ, CX * CY), ((0, 8), (1, 4)), -0.2, 0.2)), 0.5, 4.0),
        "interface_rows": draw_interface_rows(jax.random.fold_in(seeds[5], 71), 0),
        "interface_counts": draw_interface_counts(jax.random.fold_in(seeds[5], 71), 0),
    }


highest = lax.Precision.HIGHEST

def harmonic(first, second):
    return 2.0 * first * second / (first + second)

def slot_of(offset):
    return offset + REACH if offset < 0 else offset + REACH - 1

def interior(vectors, sigma_cells, storage_cells):
    width_xy = sigma_cells.shape[1]
    layers = sigma_cells.shape[0]
    position = jnp.arange(width_xy)
    result = storage_cells[None] * vectors
    for stride, at_edge in ((1, position % CX == CX - 1), (CX, position >= width_xy - CX)):
        weights = jnp.where(at_edge[None, :], 0.0, harmonic(sigma_cells, jnp.roll(sigma_cells, -stride, axis=1)))
        flow_term = weights[None] * (jnp.roll(vectors, -stride, axis=2) - vectors)
        result = result - flow_term + jnp.roll(flow_term, stride, axis=2)
    top_layer = (jnp.arange(layers) == layers - 1)[:, None]
    weights = jnp.where(top_layer, 0.0, harmonic(sigma_cells, jnp.roll(sigma_cells, -1, axis=0)))
    flow_term = weights[None] * (jnp.roll(vectors, -1, axis=1) - vectors)
    return result - flow_term + jnp.roll(flow_term, 1, axis=1)

def batch_gram(left, right):
    return jnp.einsum('sgkp,sglp->sgkl', left, right, precision=highest)

def reference(deflation, conductivity, storage, interface_rows, interface_counts):
    groups = N_COARSE
    cells = CZ * CX * CY
    vectors = deflation.reshape(N_SUB, K, groups, CZ, CX * CY).transpose(0, 2, 1, 3, 4)
    sigma_all = conductivity.reshape(N_SUB, groups, CZ, CX * CY)
    storage_all = storage.reshape(N_SUB, groups, CZ, CX * CY)
    applied = jax.vmap(jax.vmap(interior))(vectors, sigma_all, storage_all)
    own_block = jnp.einsum('sgkzx,sglzx->sgkl', vectors, applied, precision=highest)
    top_face = vectors[:, :, :, -1]
    bottom_face = vectors[:, :, :, 0]
    top_sigma = sigma_all[:, :, -1]
    bottom_sigma = sigma_all[:, :, 0]
    above = jnp.concatenate([bottom_face[:, 1:], jnp.zeros_like(bottom_face[:, :1])], axis=1)
    above_sigma = jnp.concatenate([bottom_sigma[:, 1:], jnp.zeros_like(bottom_sigma[:, :1])], axis=1)
    below = jnp.concatenate([jnp.zeros_like(top_face[:, :1]), top_face[:, :-1]], axis=1)
    below_sigma = jnp.concatenate([jnp.zeros_like(top_sigma[:, :1]), top_sigma[:, :-1]], axis=1)
    upper_weight = harmonic(top_sigma, above_sigma)[:, :, None]
    lower_weight = harmonic(bottom_sigma, below_sigma)[:, :, None]
    own_block = own_block + batch_gram(top_face * upper_weight, top_face)
    own_block = own_block + batch_gram(bottom_face * lower_weight, bottom_face)
    upper_block = -batch_gram(top_face * upper_weight, above)
    lower_block = -batch_gram(bottom_face * lower_weight, below)
    flat = vectors.reshape(N_SUB, groups, K, cells)
    flat_sigma = sigma_all.reshape(N_SUB, groups, cells)
    picked = jax.vmap(jax.vmap(lambda table, index: jnp.take(table, index.reshape(-1), axis=1)))(flat, interface_rows)
    picked = picked.reshape(N_SUB, groups, K, 2 * REACH, PAD)
    picked_sigma = jax.vmap(jax.vmap(lambda table, index: jnp.take(table, index.reshape(-1))))(flat_sigma, interface_rows)
    picked_sigma = picked_sigma.reshape(N_SUB, groups, 2 * REACH, PAD)
    column = jnp.arange(N_SUB)
    position = jnp.arange(PAD)
    lateral = [None] * (2 * REACH)
    for offset in list(range(-REACH, 0)) + list(range(1, REACH + 1)):
        slot = slot_of(offset)
        mirror = slot_of(-offset)
        valid = ((column + offset >= 0) & (column + offset < N_SUB)).astype(jnp.float32)
        partner = jnp.roll(picked[:, :, :, mirror], -offset, axis=0) * valid[:, None, None, None]
        partner_sigma = jnp.roll(picked_sigma[:, :, mirror], -offset, axis=0) * valid[:, None, None]
        own_rows = picked[:, :, :, slot]
        live = position[None, None, :] < interface_counts[:, :, slot][:, :, None]
        weights = jnp.where(live, harmonic(picked_sigma[:, :, slot], partner_sigma), 0.0)[:, :, None]
        own_block = own_block + batch_gram(own_rows * weights, own_rows)
        lateral[slot] = -batch_gram(own_rows * weights, partner)
    index_g = jnp.arange(groups)
    diag_mask = (index_g[:, None] == index_g[None, :]).astype(jnp.float32)[None, :, :, None, None]
    upper_mask = (index_g[None, :] == index_g[:, None] + 1).astype(jnp.float32)[None, :, :, None, None]
    lower_mask = (index_g[None, :] == index_g[:, None] - 1).astype(jnp.float32)[None, :, :, None, None]
    blocks = own_block[:, :, None] * diag_mask + upper_block[:, :, None] * upper_mask + lower_block[:, :, None] * lower_mask
    coarse = blocks.transpose(0, 1, 3, 2, 4).reshape(N_SUB, groups * K, groups * K)
    factor = jax.vmap(jnp.linalg.cholesky)(coarse)
    lateral_all = jnp.stack(lateral, axis=2)
    columns_all = lateral_all.transpose(0, 1, 3, 2, 4).reshape(N_SUB, groups, K, 2 * REACH * K)
    right_side = (columns_all[:, :, None] * diag_mask).reshape(N_SUB, groups, groups * K, 2 * REACH * K)

    def solve_column(lower_factor, stacked):
        return jax.vmap(lambda single: lax.linalg.triangular_solve(lower_factor, single, left_side=True, lower=True))(stacked)
    panel = jax.vmap(solve_column)(factor, right_side)
    return (factor, panel)
```

```python
import functools

import jax
import jax.numpy as jnp
from jax import lax
from jax.experimental import pallas as pl
from jax.experimental.pallas import tpu as pltpu
from jax.sharding import PartitionSpec as P

K = 64
CX = 16
REACH = 4
LANES = 128
SUB = 8
SLOTS = 2 * REACH
MESH = pl.DeviceIdType.MESH


def harmonic(first, second):
    return 2.0 * first * second / (first + second)


def offset_of(slot):
    return slot - REACH if slot < REACH else slot - REACH + 1


def halves(x):
    high = x.astype(jnp.bfloat16).astype(jnp.float32)
    return high, x - high


def split(x):
    return jnp.concatenate(halves(x), axis=0).astype(jnp.bfloat16)


def dot_nn(left, right):
    return lax.dot_general(left, right, (((1,), (0,)), ((), ())), preferred_element_type=jnp.float32)


def dot_nt(left, right):
    return lax.dot_general(left, right, (((1,), (1,)), ((), ())), preferred_element_type=jnp.float32)


def quad(g, at=0):
    return (g[:K, at : at + K] + g[K:, at : at + K]) + (g[:K, at + K : at + 2 * K] + g[K:, at + K : at + 2 * K])


def couple_kernel(
    n_sub, groups, layers, width,
    z_hbm, sig_ref, sto_ref, rows_ref, cnt_ref,
    bands_ref, lat_ref,
    z_ref, load_sem, sel_ref, lhs_ref, coef_ref, out_ref, in_ref, lay_out, lay_in, sig_out, sig_in,
    ret_out, ret_in, blk_ref, own_band,
    send_sem, recv_sem, lay_send, lay_recv, ret_send, ret_recv, band_send, band_recv,
):
    me = lax.axis_index("sub")
    level = lax.axis_index("coarse")
    cy = width // CX
    per = LANES // cy
    pad = rows_ref.shape[1]
    faces = cy * layers

    def load(c):
        return pltpu.make_async_copy(
            z_hbm.at[:, pl.ds(c * LANES, LANES)], z_ref.at[pl.ds(c * K * layers, K * layers)], load_sem.at[c]
        )

    for c in range(width // LANES):
        load(c).start()

    def layer(z):
        return jnp.concatenate(
            [z_ref[pl.ds(c * K * layers + z, K, stride=layers), :] for c in range(width // LANES)], axis=1
        )

    def reachable(slot):
        other = me + offset_of(slot)
        return jnp.logical_and(other >= 0, other < n_sub)

    barrier = pltpu.get_barrier_semaphore()
    for slot in range(SLOTS):
        @pl.when(reachable(slot))
        def _():
            pl.semaphore_signal(barrier, inc=1, device_id={"sub": me + offset_of(slot)}, device_id_type=MESH)
    for step in range(1, groups):
        pl.semaphore_signal(
            barrier, inc=1, device_id={"coarse": lax.rem(level + step, groups)}, device_id_type=MESH
        )

    row = lax.broadcasted_iota(jnp.int32, (width, 2 * LANES), 0)
    lane = lax.broadcasted_iota(jnp.int32, (width, 2 * LANES), 1)
    cell = (lane % cy) * CX + jnp.where(lane >= LANES, CX - 1, 0)
    hit = row == cell
    part = (lane % LANES) // cy
    for i in range(per):
        sel_ref[i] = jnp.where(jnp.logical_and(hit, part == i), 1.0, 0.0).astype(jnp.bfloat16)

    for c in range(width // LANES):
        load(c).wait()
    sigma = sig_ref[...]
    sigma_split = split(sigma)
    placed = []
    for i in range(per):
        t = dot_nn(sigma_split, sel_ref[i])
        placed.append(t[:layers] + t[layers:])
    for g in range(layers // per):
        total = jnp.zeros((2 * K, 2 * LANES), jnp.float32)
        sig_row = jnp.zeros((1, 2 * LANES), jnp.float32)
        for i in range(per):
            z = g * per + i
            total = total + dot_nn(split(layer(z)), sel_ref[i])
            sig_row = sig_row + placed[i][z : z + 1]
        high, low = halves(sig_row)
        sig_rows = jnp.concatenate(
            [jnp.broadcast_to(high, (SUB, 2 * LANES)), jnp.broadcast_to(low, (SUB, 2 * LANES))], axis=0
        )
        stacked = jnp.concatenate([total, sig_rows], axis=0).astype(jnp.bfloat16)
        for f in range(2):
            lhs_ref[f, :, g * LANES : (g + 1) * LANES] = stacked[:, f * LANES : (f + 1) * LANES]

    lay_out[:K] = layer(0)
    lay_out[K:] = jnp.broadcast_to(sigma[:1], (SUB, width))
    sig_out[...] = jnp.broadcast_to(sigma[layers - 1 :], (SUB, width))

    beside = jnp.minimum(me, REACH) + jnp.minimum(n_sub - 1 - me, REACH)
    pl.semaphore_wait(barrier, beside + groups - 1)

    def down():
        return pltpu.make_async_remote_copy(
            src_ref=lay_out, dst_ref=lay_in, send_sem=lay_send.at[0], recv_sem=lay_recv.at[0],
            device_id={"coarse": level - 1}, device_id_type=MESH,
        )

    def up():
        return pltpu.make_async_remote_copy(
            src_ref=sig_out, dst_ref=sig_in, send_sem=lay_send.at[1], recv_sem=lay_recv.at[1],
            device_id={"coarse": level + 1}, device_id_type=MESH,
        )

    @pl.when(level > 0)
    def _():
        down().start()

    @pl.when(level < groups - 1)
    def _():
        up().start()

    def picked_copy(slot):
        mirror = SLOTS - 1 - slot
        if slot % 2:
            src, dst = out_ref.at[slot], in_ref.at[mirror]
        else:
            src, dst = out_ref.at[slot, pl.ds(K, SUB)], in_ref.at[mirror, pl.ds(K, SUB)]
        return pltpu.make_async_remote_copy(
            src_ref=src, dst_ref=dst, send_sem=send_sem.at[slot], recv_sem=recv_sem.at[mirror],
            device_id={"sub": me + offset_of(slot)}, device_id_type=MESH,
        )

    def picked_arrival(slot):
        mirror = SLOTS - 1 - slot
        if slot % 2:
            src, dst = out_ref.at[mirror, pl.ds(K, SUB)], in_ref.at[slot, pl.ds(K, SUB)]
        else:
            src, dst = out_ref.at[mirror], in_ref.at[slot]
        return pltpu.make_async_remote_copy(
            src_ref=src, dst_ref=dst, send_sem=send_sem.at[mirror], recv_sem=recv_sem.at[slot],
            device_id={"sub": me + offset_of(slot)}, device_id_type=MESH,
        )

    face_cell = lax.broadcasted_iota(jnp.int32, (faces, pad), 0)
    for slot in (1, 7, 3, 5, 0, 2, 4, 6):
        index = lax.shift_right_logical(rows_ref[slot : slot + 1, :], CX.bit_length() - 1)
        onehot = jnp.where(face_cell == index, 1.0, 0.0).astype(jnp.bfloat16)
        picked = dot_nn(lhs_ref[0 if slot < REACH else 1], onehot)
        out_ref[slot, :K] = picked[:K] + picked[K : 2 * K]
        out_ref[slot, K:] = picked[2 * K : 2 * K + SUB] + picked[2 * K + SUB :]

        @pl.when(reachable(slot))
        def _():
            picked_copy(slot).start()

    position = lax.broadcasted_iota(jnp.int32, (layers, width), 1)
    depth = lax.broadcasted_iota(jnp.int32, (layers, width), 0)
    wx = jnp.where(position % CX == CX - 1, 0.0, harmonic(sigma, pltpu.roll(sigma, width - 1, 1)))
    wy = jnp.where(position >= width - CX, 0.0, harmonic(sigma, pltpu.roll(sigma, width - CX, 1)))
    wz = jnp.where(depth == layers - 1, 0.0, harmonic(sigma, pltpu.roll(sigma, layers - 1, 0)))
    coef_ref[0] = 0.5 * (
        sto_ref[...] + (wx + pltpu.roll(wx, 1, 1)) + (wy + pltpu.roll(wy, CX, 1)) + (wz + pltpu.roll(wz, 1, 0))
    )
    coef_ref[1] = wx
    coef_ref[2] = wy
    coef_ref[3] = wz

    def one_layer(z, gram):
        here = layer(z)
        above = layer(jnp.minimum(z + 1, layers - 1))
        applied = (
            coef_ref[0, pl.ds(z, 1), :] * here
            - coef_ref[1, pl.ds(z, 1), :] * pltpu.roll(here, width - 1, 1)
            - coef_ref[2, pl.ds(z, 1), :] * pltpu.roll(here, width - CX, 1)
            - coef_ref[3, pl.ds(z, 1), :] * above
        )
        return gram + dot_nt(split(here), split(applied))

    gram = lax.fori_loop(0, layers, one_layer, jnp.zeros((2 * K, 2 * K), jnp.float32))
    half = quad(gram)
    own = half + half.T

    @pl.when(level < groups - 1)
    def _():
        down().wait_recv()

    @pl.when(level > 0)
    def _():
        up().wait_recv()

    has_above = level < groups - 1
    has_below = level > 0
    top = layer(layers - 1)
    bottom = layer(0)
    above = jnp.where(has_above, lay_in[:K], 0.0)
    upper = jnp.where(has_above, harmonic(sigma[layers - 1 :], lay_in[K : K + 1]), 0.0)
    lower = jnp.where(has_below, harmonic(sigma[:1], sig_in[:1]), 0.0)
    both = dot_nt(split(top * upper), jnp.concatenate([split(top), split(above)], axis=0))
    own = own + quad(both)
    upper_block = -quad(both, 2 * K)
    own = own + quad(dot_nt(split(bottom * lower), split(bottom)))

    spot = lax.broadcasted_iota(jnp.int32, (1, pad), 1)

    def weights(slot):
        live = jnp.logical_and(spot < cnt_ref[0, 0, slot], reachable(slot))
        return jnp.where(live, harmonic(out_ref[slot, K : K + 1], in_ref[slot, K : K + 1]), 0.0)

    for slot in (1, 3, 5, 7):
        @pl.when(reachable(slot))
        def _():
            picked_arrival(slot).wait_recv()

        rows = out_ref[slot, :K]
        own = own + quad(dot_nt(split(rows * weights(slot)), split(rows)))

    def ret_copy(slot):
        return pltpu.make_async_remote_copy(
            src_ref=ret_out.at[slot], dst_ref=ret_in.at[SLOTS - 1 - slot],
            send_sem=ret_send.at[slot], recv_sem=ret_recv.at[SLOTS - 1 - slot],
            device_id={"sub": me + offset_of(slot)}, device_id_type=MESH,
        )

    def ret_arrival(slot):
        return pltpu.make_async_remote_copy(
            src_ref=ret_out.at[SLOTS - 1 - slot], dst_ref=ret_in.at[slot],
            send_sem=ret_send.at[SLOTS - 1 - slot], recv_sem=ret_recv.at[slot],
            device_id={"sub": me + offset_of(slot)}, device_id_type=MESH,
        )

    wide = jnp.zeros((K, LANES - K), jnp.float32)
    for slot in (0, 6, 2, 4):
        @pl.when(reachable(slot))
        def _():
            picked_arrival(slot).wait_recv()

        rows = out_ref[slot, :K]
        partner = jnp.where(reachable(slot), in_ref[slot, :K], 0.0)
        both = dot_nt(split(rows * weights(slot)), jnp.concatenate([split(rows), split(partner)], axis=0))
        own = own + quad(both)
        block = -quad(both, 2 * K)
        blk_ref[slot] = block
        ret_out[slot] = jnp.concatenate([block.T, wide], axis=1)

        @pl.when(reachable(slot))
        def _():
            ret_copy(slot).start()

    band = jnp.concatenate([own, upper_block], axis=1)
    own_band[...] = band

    def band_copy(step):
        return pltpu.make_async_remote_copy(
            src_ref=own_band, dst_ref=bands_ref.at[level],
            send_sem=band_send.at[step], recv_sem=band_recv.at[level],
            device_id={"coarse": lax.rem(level + step, groups)}, device_id_type=MESH,
        )

    for step in range(1, groups):
        band_copy(step).start()
    bands_ref[level] = band
    for slot in range(SLOTS):
        if slot % 2:
            @pl.when(reachable(slot))
            def _():
                ret_arrival(slot).wait_recv()

            blk_ref[slot] = jnp.where(reachable(slot), ret_in[slot, :, :K], 0.0)
    for pair in range(SLOTS // 2):
        lat_ref[:, pair * 2 * K : (pair + 1) * 2 * K] = jnp.concatenate(
            [blk_ref[2 * pair], blk_ref[2 * pair + 1]], axis=1
        )
    for step in range(1, groups):
        source = lax.rem(level + groups - step, groups)
        pltpu.make_async_remote_copy(
            src_ref=own_band, dst_ref=bands_ref.at[source],
            send_sem=band_send.at[step], recv_sem=band_recv.at[source],
            device_id={"coarse": source}, device_id_type=MESH,
        ).wait_recv()
    for step in range(1, groups):
        band_copy(step).wait_send()
    for slot in range(SLOTS):
        @pl.when(reachable(slot))
        def _():
            picked_copy(slot).wait_send()
            if slot % 2 == 0:
                ret_copy(slot).wait_send()

    @pl.when(level > 0)
    def _():
        down().wait_send()

    @pl.when(level < groups - 1)
    def _():
        up().wait_send()


def spread(x, at):
    return jnp.broadcast_to(x[at : at + 1, :], x.shape)


def column(x, at):
    return jnp.broadcast_to(x[:, at : at + 1], (x.shape[0], LANES))


def eliminate(left, right):
    left, right = list(left), list(right)
    below = lax.broadcasted_iota(jnp.int32, (SUB, LANES), 0)
    for p in range(K // SUB):
        cols = [[column(left[g], p * SUB + j) for j in range(SUB)] for g in range(p, K // SUB)]
        head = cols[0]
        a, b = left[p], right[p]
        inverses, above = [], []
        for j in range(SUB):
            inverse = 1.0 / spread(head[j], j)
            inverses.append(inverse)
            scale = jnp.where(below > j, head[j] * inverse, 0.0)
            entries = {k: spread(head[k], j) for k in range(j + 1, SUB)}
            above.append(entries)
            for k in range(j + 1, SUB):
                head[k] = head[k] - scale * entries[k]
            a = a - scale * spread(a, j)
            b = b - scale * spread(b, j)
        left[p], right[p] = a, b
        rows_a = [spread(a, j) for j in range(SUB)]
        rows_b = [spread(b, j) for j in range(SUB)]
        for g in range(p + 1, K // SUB):
            tail = cols[g - p]
            la, lb = left[g], right[g]
            for j in range(SUB):
                scale = tail[j] * inverses[j]
                for k in range(j + 1, SUB):
                    tail[k] = tail[k] - scale * above[j][k]
                la = la - scale * rows_a[j]
                lb = lb - scale * rows_b[j]
            left[g], right[g] = la, lb
        for j in range(SUB):
            root = lax.rsqrt(spread_pivot(a, p * SUB + j, j))
            left[p] = jnp.where(below == j, left[p] * root, left[p])
            right[p] = jnp.where(below == j, right[p] * root, right[p])
    return left, right


def spread_pivot(x, lane, row):
    return jnp.broadcast_to(x[row : row + 1, lane : lane + 1], x.shape)


def exact_nn(left, right):
    return lax.dot_general(
        left, right, (((1,), (0,)), ((), ())), preferred_element_type=jnp.float32,
        precision=lax.Precision.HIGHEST,
    )


def exact_tn(left, right):
    return lax.dot_general(
        left, right, (((0,), (0,)), ((), ())), preferred_element_type=jnp.float32,
        precision=lax.Precision.HIGHEST,
    )


def factor_kernel(groups, bands_ref, lat_ref, factor_ref, panel_ref, low_ref, inv_ref, turn_ref, schur_ref):
    level = lax.axis_index("coarse")
    row = lax.broadcasted_iota(jnp.int32, (K, LANES), 0)
    lane = lax.broadcasted_iota(jnp.int32, (K, LANES), 1)
    eye = jnp.where(row == lane, 1.0, 0.0)
    schur_ref[...] = jnp.zeros_like(schur_ref)

    def one_block(k, carry):
        start = bands_ref[k] - schur_ref[...]
        tiles = [start[g * SUB : (g + 1) * SUB] for g in range(K // SUB)]
        ones = [eye[g * SUB : (g + 1) * SUB] for g in range(K // SUB)]
        left, right = eliminate(tiles, ones)
        left = jnp.concatenate(left, axis=0)
        right = jnp.concatenate(right, axis=0)
        left = jnp.where(lane >= row, left, 0.0)
        low_ref[k] = left
        inv_ref[k] = right
        turn = left[:, K:]
        turn_ref[k] = turn
        schur_ref[:, :K] = exact_tn(turn, turn)
        return carry

    lax.fori_loop(0, groups, one_block, 0)

    factor_ref[0] = jnp.zeros_like(factor_ref[0])
    last = jnp.zeros((K, panel_ref.shape[3]), jnp.float32)
    for k in range(groups):
        lower = low_ref[k].T
        factor_ref[0, k * K : (k + 1) * K, k * K : (k + 1) * K] = lower[:K]
        if k + 1 < groups:
            factor_ref[0, (k + 1) * K : (k + 2) * K, k * K : (k + 1) * K] = lower[K:]
        right = jnp.where(level == k, lat_ref[...], 0.0)
        if k:
            right = right - exact_tn(turn_ref[k - 1], last)
        last = exact_nn(inv_ref[k, :, :K], right)
        panel_ref[0, 0, k * K : (k + 1) * K, :] = last


def body(n_sub, groups, deflation, conductivity, storage, interface_rows, interface_counts):
    layers, width = deflation.shape[2], deflation.shape[3]
    pad = interface_rows.shape[3]
    faces = width // CX * layers
    f32 = jnp.float32
    vmem = pl.BlockSpec(memory_space=pltpu.VMEM)
    dma = pltpu.SemaphoreType.DMA
    bands, lateral = pl.pallas_call(
        functools.partial(couple_kernel, n_sub, groups, layers, width),
        out_shape=(
            jax.ShapeDtypeStruct((groups, K, 2 * K), f32),
            jax.ShapeDtypeStruct((K, SLOTS * K), f32),
        ),
        in_specs=[pl.BlockSpec(memory_space=pl.ANY), vmem, vmem, vmem, pl.BlockSpec(memory_space=pltpu.SMEM)],
        out_specs=(vmem, vmem),
        scratch_shapes=[
            pltpu.VMEM((width // LANES * K * layers, LANES), f32),
            dma((width // LANES,)),
            pltpu.VMEM((LANES * CX // width, width, 2 * LANES), jnp.bfloat16),
            pltpu.VMEM((2, 2 * K + 2 * SUB, faces), jnp.bfloat16),
            pltpu.VMEM((4, layers, width), f32),
            pltpu.VMEM((SLOTS, K + SUB, pad), f32),
            pltpu.VMEM((SLOTS, K + SUB, pad), f32),
            pltpu.VMEM((K + SUB, width), f32),
            pltpu.VMEM((K + SUB, width), f32),
            pltpu.VMEM((SUB, width), f32),
            pltpu.VMEM((SUB, width), f32),
            pltpu.VMEM((SLOTS, K, LANES), f32),
            pltpu.VMEM((SLOTS, K, LANES), f32),
            pltpu.VMEM((SLOTS, K, K), f32),
            pltpu.VMEM((K, 2 * K), f32),
            dma((SLOTS,)), dma((SLOTS,)), dma((2,)), dma((2,)),
            dma((SLOTS,)), dma((SLOTS,)), dma((groups,)), dma((groups,)),
        ],
        compiler_params=pltpu.CompilerParams(
            collective_id=0, has_side_effects=True, vmem_limit_bytes=40 * 1024 * 1024
        ),
        name="couple",
    )(
        deflation.reshape(K * layers, width), conductivity[0], storage[0],
        interface_rows[0, 0], interface_counts,
    )
    return pl.pallas_call(
        functools.partial(factor_kernel, groups),
        out_shape=(
            jax.ShapeDtypeStruct((1, groups * K, groups * K), f32),
            jax.ShapeDtypeStruct((1, 1, groups * K, SLOTS * K), f32),
        ),
        in_specs=[vmem, vmem],
        out_specs=(vmem, vmem),
        scratch_shapes=[
            pltpu.VMEM((groups, K, LANES), f32),
            pltpu.VMEM((groups, K, LANES), f32),
            pltpu.VMEM((groups, K, K), f32),
            pltpu.VMEM((K, LANES), f32),
        ],
        compiler_params=pltpu.CompilerParams(vmem_limit_bytes=40 * 1024 * 1024),
        name="factor",
    )(bands, lateral)


def solution(mesh):
    placed = (
        P("sub", None, "coarse", None),
        P("sub", "coarse", None),
        P("sub", "coarse", None),
        P("sub", "coarse", None, None),
        P("sub", "coarse", None),
    )
    return jax.shard_map(
        functools.partial(body, mesh.shape["sub"], mesh.shape["coarse"]),
        mesh=mesh,
        in_specs=placed,
        out_specs=(P("sub", None, None), P("sub", "coarse", None, None)),
        check_vma=False,
    )
```

```python
import functools

import jax
import jax.numpy as jnp
from jax import lax
from jax.experimental import pallas as pl
from jax.experimental.pallas import tpu as pltpu
from jax.sharding import PartitionSpec as P

K = 64
CX = 16
REACH = 4
LANES = 128
SUB = 8
SLOTS = 2 * REACH
MESH = pl.DeviceIdType.MESH


def harmonic(first, second):
    return 2.0 * first * second / (first + second)


def offset_of(slot):
    return slot - REACH if slot < REACH else slot - REACH + 1


def halves(x):
    high = x.astype(jnp.bfloat16).astype(jnp.float32)
    return high, x - high


def split(x):
    return jnp.concatenate(halves(x), axis=0).astype(jnp.bfloat16)


def dot_nn(left, right):
    return lax.dot_general(left, right, (((1,), (0,)), ((), ())), preferred_element_type=jnp.float32)


def dot_nt(left, right):
    return lax.dot_general(left, right, (((1,), (1,)), ((), ())), preferred_element_type=jnp.float32)


def quad(g, at=0):
    return (g[:K, at : at + K] + g[K:, at : at + K]) + (g[:K, at + K : at + 2 * K] + g[K:, at + K : at + 2 * K])


def couple_kernel(
    n_sub, groups, layers, width,
    z_hbm, sig_hbm, sto_hbm, rows_hbm, cnt_hbm,
    bands_ref, lat_ref,
    z_ref, load_sem, sig_ref, sto_ref, rows_ref, cnt_ref, small_sem, sel_ref, lhs_ref, coef_ref, out_ref, in_ref, psig_out, psig_in, lay_out, lay_in, sig_out, sig_in,
    ret_out, ret_in, blk_ref, wgt_ref, own_band,
    send_sem, recv_sem, psig_send, psig_recv, lay_send, lay_recv, ret_send, ret_recv, band_send, band_recv,
):
    me = lax.axis_index("sub")
    level = lax.axis_index("coarse")
    cy = width // CX
    per = LANES // cy
    pad = rows_ref.shape[1]
    faces = cy * layers

    def load(c):
        return pltpu.make_async_copy(
            z_hbm.at[:, pl.ds(c * LANES, LANES)], z_ref.at[pl.ds(c * K * layers, K * layers)], load_sem.at[c]
        )

    small = [
        pltpu.make_async_copy(src, dst, small_sem.at[i])
        for i, (src, dst) in enumerate(
            ((sig_hbm, sig_ref), (rows_hbm, rows_ref), (sto_hbm, sto_ref), (cnt_hbm, cnt_ref))
        )
    ]
    for copy in small:
        copy.start()
    for c in range(width // LANES):
        load(c).start()

    def layer(z):
        return jnp.concatenate(
            [z_ref[pl.ds(c * K * layers + z, K, stride=layers), :] for c in range(width // LANES)], axis=1
        )

    def reachable(slot):
        other = me + offset_of(slot)
        return jnp.logical_and(other >= 0, other < n_sub)

    barrier = pltpu.get_barrier_semaphore()
    for slot in range(SLOTS):
        @pl.when(reachable(slot))
        def _():
            pl.semaphore_signal(barrier, inc=1, device_id={"sub": me + offset_of(slot)}, device_id_type=MESH)
    for step in range(1, groups):
        pl.semaphore_signal(
            barrier, inc=1, device_id={"coarse": lax.rem(level + step, groups)}, device_id_type=MESH
        )

    row = lax.broadcasted_iota(jnp.int32, (width, 2 * LANES), 0)
    lane = lax.broadcasted_iota(jnp.int32, (width, 2 * LANES), 1)
    cell = (lane % cy) * CX + jnp.where(lane >= LANES, CX - 1, 0)
    hit = row == cell
    part = (lane % LANES) // cy
    for i in range(per):
        sel_ref[i] = jnp.where(jnp.logical_and(hit, part == i), 1.0, 0.0).astype(jnp.bfloat16)

    for copy in small:
        copy.wait()
    sigma = sig_ref[...]
    sigma_split = split(sigma)
    placed = []
    for i in range(per):
        t = dot_nn(sigma_split, sel_ref[i])
        placed.append(t[:layers] + t[layers:])
    for c in range(width // LANES):
        load(c).wait()
    for g in range(layers // per):
        total = jnp.zeros((2 * K, 2 * LANES), jnp.float32)
        sig_row = jnp.zeros((1, 2 * LANES), jnp.float32)
        for i in range(per):
            z = g * per + i
            total = total + dot_nn(split(layer(z)), sel_ref[i])
            sig_row = sig_row + placed[i][z : z + 1]
        high, low = halves(sig_row)
        sig_rows = jnp.concatenate(
            [jnp.broadcast_to(high, (SUB, 2 * LANES)), jnp.broadcast_to(low, (SUB, 2 * LANES))], axis=0
        )
        stacked = jnp.concatenate([total, sig_rows], axis=0).astype(jnp.bfloat16)
        for f in range(2):
            lhs_ref[f, :, g * LANES : (g + 1) * LANES] = stacked[:, f * LANES : (f + 1) * LANES]

    lay_out[:K] = layer(0)
    lay_out[K:] = jnp.broadcast_to(sigma[:1], (SUB, width))
    sig_out[...] = jnp.broadcast_to(sigma[layers - 1 :], (SUB, width))

    beside = jnp.minimum(me, REACH) + jnp.minimum(n_sub - 1 - me, REACH)
    pl.semaphore_wait(barrier, beside + groups - 1)

    def down():
        return pltpu.make_async_remote_copy(
            src_ref=lay_out, dst_ref=lay_in, send_sem=lay_send.at[0], recv_sem=lay_recv.at[0],
            device_id={"coarse": level - 1}, device_id_type=MESH,
        )

    def up():
        return pltpu.make_async_remote_copy(
            src_ref=sig_out, dst_ref=sig_in, send_sem=lay_send.at[1], recv_sem=lay_recv.at[1],
            device_id={"coarse": level + 1}, device_id_type=MESH,
        )

    @pl.when(level > 0)
    def _():
        down().start()

    @pl.when(level < groups - 1)
    def _():
        up().start()

    def picked_copy(slot):
        mirror = SLOTS - 1 - slot
        return pltpu.make_async_remote_copy(
            src_ref=out_ref.at[slot], dst_ref=in_ref.at[mirror // 2],
            send_sem=send_sem.at[slot // 2], recv_sem=recv_sem.at[mirror // 2],
            device_id={"sub": me + offset_of(slot)}, device_id_type=MESH,
        )

    def sigma_copy(slot):
        mirror = SLOTS - 1 - slot
        return pltpu.make_async_remote_copy(
            src_ref=psig_out.at[slot], dst_ref=psig_in.at[mirror],
            send_sem=psig_send.at[slot], recv_sem=psig_recv.at[mirror],
            device_id={"sub": me + offset_of(slot)}, device_id_type=MESH,
        )

    face_cell = lax.broadcasted_iota(jnp.int32, (faces, pad), 0)
    for batch in ((1, 7), (3, 5), (0, 2, 4, 6)):
        for slot in batch:
            index = lax.shift_right_logical(rows_ref[slot : slot + 1, :], CX.bit_length() - 1)
            onehot = jnp.where(face_cell == index, 1.0, 0.0).astype(jnp.bfloat16)
            picked = dot_nn(lhs_ref[0 if slot < REACH else 1], onehot)
            out_ref[slot] = picked[:K] + picked[K : 2 * K]
            psig_out[slot] = picked[2 * K : 2 * K + SUB] + picked[2 * K + SUB :]
        for slot in batch:
            @pl.when(reachable(slot))
            def _():
                if slot % 2:
                    picked_copy(slot).start()
                sigma_copy(slot).start()

    position = lax.broadcasted_iota(jnp.int32, (layers, width), 1)
    depth = lax.broadcasted_iota(jnp.int32, (layers, width), 0)
    wx = jnp.where(position % CX == CX - 1, 0.0, harmonic(sigma, pltpu.roll(sigma, width - 1, 1)))
    wy = jnp.where(position >= width - CX, 0.0, harmonic(sigma, pltpu.roll(sigma, width - CX, 1)))
    wz = jnp.where(depth == layers - 1, 0.0, harmonic(sigma, pltpu.roll(sigma, layers - 1, 0)))
    coef_ref[0] = 0.5 * (
        sto_ref[...] + (wx + pltpu.roll(wx, 1, 1)) + (wy + pltpu.roll(wy, CX, 1)) + (wz + pltpu.roll(wz, 1, 0))
    )
    coef_ref[1] = wx
    coef_ref[2] = wy
    coef_ref[3] = wz

    def some_layers(step, gram):
        start = step * per
        cells = [layer(start + i) for i in range(per)]
        cells.append(layer(jnp.minimum(start + per, layers - 1)))
        lefts, rights = [], []
        for i in range(per):
            z = start + i
            here = cells[i]
            applied = (
                coef_ref[0, pl.ds(z, 1), :] * here
                - coef_ref[1, pl.ds(z, 1), :] * pltpu.roll(here, width - 1, 1)
                - coef_ref[2, pl.ds(z, 1), :] * pltpu.roll(here, width - CX, 1)
                - coef_ref[3, pl.ds(z, 1), :] * cells[i + 1]
            )
            lefts.append(split(here))
            rights.append(split(applied))
        return gram + dot_nt(jnp.concatenate(lefts, axis=1), jnp.concatenate(rights, axis=1))

    gram = lax.fori_loop(0, layers // per, some_layers, jnp.zeros((2 * K, 2 * K), jnp.float32))
    half = quad(gram)
    own = half + half.T

    @pl.when(level < groups - 1)
    def _():
        down().wait_recv()

    @pl.when(level > 0)
    def _():
        up().wait_recv()

    for slot in range(SLOTS):
        @pl.when(reachable(slot))
        def _():
            sigma_copy(SLOTS - 1 - slot).wait_recv()

    has_above = level < groups - 1
    has_below = level > 0
    top = layer(layers - 1)
    bottom = layer(0)
    above = jnp.where(has_above, lay_in[:K], 0.0)
    upper = jnp.where(has_above, harmonic(sigma[layers - 1 :], lay_in[K : K + 1]), 0.0)
    lower = jnp.where(has_below, harmonic(sigma[:1], sig_in[:1]), 0.0)
    top_weighted = split(top * upper)
    upper_block = -quad(dot_nt(top_weighted, split(above)))
    spot = lax.broadcasted_iota(jnp.int32, (1, pad), 1)
    lefts = [top_weighted, split(bottom * lower)]
    rights = [split(top), split(bottom)]
    for slot in range(SLOTS):
        live = jnp.logical_and(spot < cnt_ref[0, 0, slot], reachable(slot))
        weight = jnp.where(live, harmonic(psig_out[slot, :1], psig_in[slot, :1]), 0.0)
        rows = out_ref[slot]
        lefts.append(split(rows * weight))
        rights.append(split(rows))
        if slot % 2 == 0:
            wgt_ref[slot // 2] = lefts[-1]
    own = own + quad(dot_nt(jnp.concatenate(lefts, axis=1), jnp.concatenate(rights, axis=1)))

    band = jnp.concatenate([own, upper_block], axis=1)
    own_band[...] = band

    def band_copy(step):
        return pltpu.make_async_remote_copy(
            src_ref=own_band, dst_ref=bands_ref.at[level],
            send_sem=band_send.at[step], recv_sem=band_recv.at[level],
            device_id={"coarse": lax.rem(level + step, groups)}, device_id_type=MESH,
        )

    for step in range(1, groups):
        band_copy(step).start()
    bands_ref[level] = band

    def ret_copy(slot):
        return pltpu.make_async_remote_copy(
            src_ref=ret_out.at[slot], dst_ref=ret_in.at[SLOTS - 1 - slot],
            send_sem=ret_send.at[slot], recv_sem=ret_recv.at[SLOTS - 1 - slot],
            device_id={"sub": me + offset_of(slot)}, device_id_type=MESH,
        )

    def ret_arrival(slot):
        return pltpu.make_async_remote_copy(
            src_ref=ret_out.at[SLOTS - 1 - slot], dst_ref=ret_in.at[slot],
            send_sem=ret_send.at[SLOTS - 1 - slot], recv_sem=ret_recv.at[slot],
            device_id={"sub": me + offset_of(slot)}, device_id_type=MESH,
        )

    for slot in range(0, SLOTS, 2):
        @pl.when(reachable(slot))
        def _():
            picked_copy(SLOTS - 1 - slot).wait_recv()

    wide = jnp.zeros((K, LANES - K), jnp.float32)
    for slot in range(0, SLOTS, 2):
        partner = jnp.where(reachable(slot), in_ref[slot // 2], 0.0)
        block = -quad(dot_nt(wgt_ref[slot // 2], split(partner)))
        blk_ref[slot] = block
        ret_out[slot] = jnp.concatenate([block.T, wide], axis=1)
    for slot in range(0, SLOTS, 2):
        @pl.when(reachable(slot))
        def _():
            ret_copy(slot).start()

    for slot in range(SLOTS):
        if slot % 2:
            @pl.when(reachable(slot))
            def _():
                ret_arrival(slot).wait_recv()

            blk_ref[slot] = jnp.where(reachable(slot), ret_in[slot, :, :K], 0.0)
    for pair in range(SLOTS // 2):
        lat_ref[:, pair * 2 * K : (pair + 1) * 2 * K] = jnp.concatenate(
            [blk_ref[2 * pair], blk_ref[2 * pair + 1]], axis=1
        )
    for step in range(1, groups):
        source = lax.rem(level + groups - step, groups)
        pltpu.make_async_remote_copy(
            src_ref=own_band, dst_ref=bands_ref.at[source],
            send_sem=band_send.at[step], recv_sem=band_recv.at[source],
            device_id={"coarse": source}, device_id_type=MESH,
        ).wait_recv()
    for step in range(1, groups):
        band_copy(step).wait_send()
    for slot in range(SLOTS):
        @pl.when(reachable(slot))
        def _():
            sigma_copy(slot).wait_send()
            if slot % 2:
                picked_copy(slot).wait_send()
            else:
                ret_copy(slot).wait_send()

    @pl.when(level > 0)
    def _():
        down().wait_send()

    @pl.when(level < groups - 1)
    def _():
        up().wait_send()


def spread(x, at):
    return jnp.broadcast_to(x[at : at + 1, :], x.shape)


def column(x, at):
    return jnp.broadcast_to(x[:, at : at + 1], (x.shape[0], LANES))


def eliminate(left, right):
    left, right = list(left), list(right)
    below = lax.broadcasted_iota(jnp.int32, (SUB, LANES), 0)
    for p in range(K // SUB):
        cols = [[column(left[g], p * SUB + j) for j in range(SUB)] for g in range(p, K // SUB)]
        head = cols[0]
        a, b = left[p], right[p]
        inverses, above = [], []
        for j in range(SUB):
            inverse = 1.0 / spread(head[j], j)
            inverses.append(inverse)
            scale = jnp.where(below > j, head[j], 0.0) * inverse
            entries = {k: spread(head[k], j) for k in range(j + 1, SUB)}
            above.append(entries)
            for k in range(j + 1, SUB):
                head[k] = head[k] - scale * entries[k]
            a = a - scale * spread(a, j)
            b = b - scale * spread(b, j)
        left[p], right[p] = a, b
        rows_a = [spread(a, j) for j in range(SUB)]
        rows_b = [spread(b, j) for j in range(SUB)]
        for g in range(p + 1, K // SUB):
            tail = cols[g - p]
            la, lb = left[g], right[g]
            for j in range(SUB):
                scale = tail[j] * inverses[j]
                for k in range(j + 1, SUB):
                    tail[k] = tail[k] - scale * above[j][k]
                la = la - scale * rows_a[j]
                lb = lb - scale * rows_b[j]
            left[g], right[g] = la, lb
        for j in range(SUB):
            root = lax.rsqrt(spread_pivot(a, p * SUB + j, j))
            left[p] = jnp.where(below == j, left[p] * root, left[p])
            right[p] = jnp.where(below == j, right[p] * root, right[p])
    return left, right


def spread_pivot(x, lane, row):
    return jnp.broadcast_to(x[row : row + 1, lane : lane + 1], x.shape)


def thirds(x):
    high, rest = halves(x)
    middle, low = halves(rest)
    return high, middle, low


def exact_tn(left, right):
    a, b, c = thirds(left)
    d, e, f = thirds(right)
    return lax.dot_general(
        jnp.concatenate([a, a, b, b, a, c], axis=0).astype(jnp.bfloat16),
        jnp.concatenate([d, e, d, e, f, d], axis=0).astype(jnp.bfloat16),
        (((0,), (0,)), ((), ())), preferred_element_type=jnp.float32,
    )


def factor_kernel(
    groups, bands_ref, lat_ref, factor_ref, panel_ref, low_ref, inv_ref, turn_ref, schur_ref, last_ref
):
    level = lax.axis_index("coarse")
    row = lax.broadcasted_iota(jnp.int32, (K, LANES), 0)
    lane = lax.broadcasted_iota(jnp.int32, (K, LANES), 1)
    eye = jnp.where(row == lane, 1.0, 0.0)
    schur_ref[...] = jnp.zeros_like(schur_ref)
    last_ref[...] = jnp.zeros_like(last_ref)
    low_ref[0] = jnp.zeros_like(low_ref[0])
    inv_ref[0] = jnp.zeros_like(inv_ref[0])
    turn_ref[0] = jnp.zeros_like(turn_ref[0])

    def panel_block(k, before):
        right = jnp.where(level == k, lat_ref[...], 0.0) - exact_tn(turn_ref[before], last_ref[...])
        return exact_tn(inv_ref[jnp.maximum(k, 0)], right)

    def one_block(k, carry):
        done = jnp.maximum(k - 1, 0)
        last = panel_block(k - 1, jnp.maximum(k - 2, 0))
        start = bands_ref[k] - schur_ref[...]
        tiles = [start[g * SUB : (g + 1) * SUB] for g in range(K // SUB)]
        ones = [eye[g * SUB : (g + 1) * SUB] for g in range(K // SUB)]
        left, right = eliminate(tiles, ones)
        left = jnp.concatenate(left, axis=0)
        right = jnp.concatenate(right, axis=0)
        left = jnp.where(lane >= row, left, 0.0)
        turn = left[:, K:]
        last_ref[...] = last
        panel_ref[0, 0, pl.ds(pl.multiple_of(done * K, K), K), :] = last
        low_ref[k] = left.T
        inv_ref[k] = right.T[:K]
        turn_ref[k] = turn
        schur_ref[:, :K] = exact_tn(turn, turn)
        return carry

    factor_ref[0] = jnp.zeros_like(factor_ref[0])
    lax.fori_loop(0, groups, one_block, 0)
    panel_ref[0, 0, (groups - 1) * K :, :] = panel_block(groups - 1, groups - 2)
    for k in range(groups):
        factor_ref[0, k * K : (k + 1) * K, k * K : (k + 1) * K] = low_ref[k, :K]
        if k + 1 < groups:
            factor_ref[0, (k + 1) * K : (k + 2) * K, k * K : (k + 1) * K] = low_ref[k, K:]


def body(n_sub, groups, deflation, conductivity, storage, interface_rows, interface_counts):
    layers, width = deflation.shape[2], deflation.shape[3]
    pad = interface_rows.shape[3]
    faces = width // CX * layers
    f32 = jnp.float32
    vmem = pl.BlockSpec(memory_space=pltpu.VMEM)
    dma = pltpu.SemaphoreType.DMA
    bands, lateral = pl.pallas_call(
        functools.partial(couple_kernel, n_sub, groups, layers, width),
        out_shape=(
            jax.ShapeDtypeStruct((groups, K, 2 * K), f32),
            jax.ShapeDtypeStruct((K, SLOTS * K), f32),
        ),
        in_specs=[pl.BlockSpec(memory_space=pltpu.HBM)] * 5,
        out_specs=(vmem, vmem),
        scratch_shapes=[
            pltpu.VMEM((width // LANES * K * layers, LANES), f32),
            dma((width // LANES,)),
            pltpu.VMEM((layers, width), f32),
            pltpu.VMEM((layers, width), f32),
            pltpu.VMEM((SLOTS, pad), jnp.int32),
            pltpu.SMEM((1, 1, SLOTS), jnp.int32),
            dma((4,)),
            pltpu.VMEM((LANES * CX // width, width, 2 * LANES), jnp.bfloat16),
            pltpu.VMEM((2, 2 * K + 2 * SUB, faces), jnp.bfloat16),
            pltpu.VMEM((4, layers, width), f32),
            pltpu.VMEM((SLOTS, K, pad), f32),
            pltpu.VMEM((REACH, K, pad), f32),
            pltpu.VMEM((SLOTS, SUB, pad), f32),
            pltpu.VMEM((SLOTS, SUB, pad), f32),
            pltpu.VMEM((K + SUB, width), f32),
            pltpu.VMEM((K + SUB, width), f32),
            pltpu.VMEM((SUB, width), f32),
            pltpu.VMEM((SUB, width), f32),
            pltpu.VMEM((SLOTS, K, LANES), f32),
            pltpu.VMEM((SLOTS, K, LANES), f32),
            pltpu.VMEM((SLOTS, K, K), f32),
            pltpu.VMEM((REACH, 2 * K, pad), jnp.bfloat16),
            pltpu.VMEM((K, 2 * K), f32),
            dma((REACH,)), dma((REACH,)), dma((SLOTS,)), dma((SLOTS,)), dma((2,)), dma((2,)),
            dma((SLOTS,)), dma((SLOTS,)), dma((groups,)), dma((groups,)),
        ],
        compiler_params=pltpu.CompilerParams(
            collective_id=0, has_side_effects=True, vmem_limit_bytes=40 * 1024 * 1024
        ),
        name="couple",
    )(
        *(
            pltpu.with_memory_space_constraint(x, pltpu.HBM)
            for x in (
                deflation.reshape(K * layers, width), conductivity[0], storage[0],
                interface_rows[0, 0], interface_counts,
            )
        )
    )
    return pl.pallas_call(
        functools.partial(factor_kernel, groups),
        out_shape=(
            jax.ShapeDtypeStruct((1, groups * K, groups * K), f32),
            jax.ShapeDtypeStruct((1, 1, groups * K, SLOTS * K), f32),
        ),
        in_specs=[vmem, vmem],
        out_specs=(vmem, vmem),
        scratch_shapes=[
            pltpu.VMEM((groups, 2 * K, K), f32),
            pltpu.VMEM((groups, K, K), f32),
            pltpu.VMEM((groups, K, K), f32),
            pltpu.VMEM((K, LANES), f32),
            pltpu.VMEM((K, SLOTS * K), f32),
        ],
        compiler_params=pltpu.CompilerParams(vmem_limit_bytes=40 * 1024 * 1024),
        name="factor",
    )(bands, lateral)


def solution(mesh):
    placed = (
        P("sub", None, "coarse", None),
        P("sub", "coarse", None),
        P("sub", "coarse", None),
        P("sub", "coarse", None, None),
        P("sub", "coarse", None),
    )
    return jax.shard_map(
        functools.partial(body, mesh.shape["sub"], mesh.shape["coarse"]),
        mesh=mesh,
        in_specs=placed,
        out_specs=(P("sub", None, None), P("sub", "coarse", None, None)),
        check_vma=False,
    )
```

```python
import functools

import jax
import jax.numpy as jnp
from jax import lax
from jax.experimental import pallas as pl
from jax.experimental.pallas import tpu as pltpu
from jax.sharding import PartitionSpec as P

K = 64
CX = 16
REACH = 4
LANES = 128
SUB = 8
SLOTS = 2 * REACH
MESH = pl.DeviceIdType.MESH


def harmonic(first, second):
    return 2.0 * first * second / (first + second)


def offset_of(slot):
    return slot - REACH if slot < REACH else slot - REACH + 1


def halves(x):
    high = x.astype(jnp.bfloat16).astype(jnp.float32)
    return high, x - high


def split(x):
    return jnp.concatenate(halves(x), axis=0).astype(jnp.bfloat16)


def dot_nn(left, right):
    return lax.dot_general(left, right, (((1,), (0,)), ((), ())), preferred_element_type=jnp.float32)


def dot_nt(left, right):
    return lax.dot_general(left, right, (((1,), (1,)), ((), ())), preferred_element_type=jnp.float32)


def quad(g, at=0):
    return (g[:K, at : at + K] + g[K:, at : at + K]) + (g[:K, at + K : at + 2 * K] + g[K:, at + K : at + 2 * K])


def couple_kernel(
    n_sub, groups, layers, width,
    z_hbm, sig_hbm, sto_hbm, rows_hbm, cnt_hbm,
    bands_ref, lat_ref,
    z_ref, load_sem, sig_ref, sto_ref, rows_ref, cnt_ref, small_sem, sel_ref, lhs_ref, coef_ref, out_ref, in_ref, psig_out, psig_in, lay_out, lay_in, sig_out, sig_in,
    ret_out, ret_in, blk_ref, wgt_ref, hot_ref, own_band,
    send_sem, recv_sem, psig_send, psig_recv, lay_send, lay_recv, ret_send, ret_recv, band_send, band_recv,
):
    me = lax.axis_index("sub")
    level = lax.axis_index("coarse")
    cy = width // CX
    per = LANES // cy
    pad = rows_ref.shape[1]
    faces = cy * layers

    def load(c):
        return pltpu.make_async_copy(
            z_hbm.at[:, pl.ds(c * LANES, LANES)], z_ref.at[pl.ds(c * K * layers, K * layers)], load_sem.at[c]
        )

    small = [
        pltpu.make_async_copy(src, dst, small_sem.at[i])
        for i, (src, dst) in enumerate(
            ((sig_hbm, sig_ref), (rows_hbm, rows_ref), (sto_hbm, sto_ref), (cnt_hbm, cnt_ref))
        )
    ]
    for copy in small:
        copy.start()
    for c in range(width // LANES):
        load(c).start()

    def layer(z):
        return jnp.concatenate(
            [z_ref[pl.ds(c * K * layers + z, K, stride=layers), :] for c in range(width // LANES)], axis=1
        )

    def reachable(slot):
        other = me + offset_of(slot)
        return jnp.logical_and(other >= 0, other < n_sub)

    barrier = pltpu.get_barrier_semaphore()
    for slot in range(SLOTS):
        @pl.when(reachable(slot))
        def _():
            pl.semaphore_signal(barrier, inc=1, device_id={"sub": me + offset_of(slot)}, device_id_type=MESH)
    for step in range(1, groups):
        pl.semaphore_signal(
            barrier, inc=1, device_id={"coarse": lax.rem(level + step, groups)}, device_id_type=MESH
        )

    row = lax.broadcasted_iota(jnp.int32, (width, 2 * LANES), 0)
    lane = lax.broadcasted_iota(jnp.int32, (width, 2 * LANES), 1)
    cell = (lane % cy) * CX + jnp.where(lane >= LANES, CX - 1, 0)
    hit = row == cell
    part = (lane % LANES) // cy
    for i in range(per):
        sel_ref[i] = jnp.where(jnp.logical_and(hit, part == i), 1.0, 0.0).astype(jnp.bfloat16)

    for copy in small:
        copy.wait()
    sigma = sig_ref[...]
    sigma_split = split(sigma)
    placed = []
    for i in range(per):
        t = dot_nn(sigma_split, sel_ref[i])
        placed.append(t[:layers] + t[layers:])
    position = lax.broadcasted_iota(jnp.int32, (layers, width), 1)
    depth = lax.broadcasted_iota(jnp.int32, (layers, width), 0)
    wx = jnp.where(position % CX == CX - 1, 0.0, harmonic(sigma, pltpu.roll(sigma, width - 1, 1)))
    wy = jnp.where(position >= width - CX, 0.0, harmonic(sigma, pltpu.roll(sigma, width - CX, 1)))
    wz = jnp.where(depth == layers - 1, 0.0, harmonic(sigma, pltpu.roll(sigma, layers - 1, 0)))
    coef_ref[0] = 0.5 * (
        sto_ref[...] + (wx + pltpu.roll(wx, 1, 1)) + (wy + pltpu.roll(wy, CX, 1)) + (wz + pltpu.roll(wz, 1, 0))
    )
    coef_ref[1] = wx
    coef_ref[2] = wy
    coef_ref[3] = wz

    face_cell = lax.broadcasted_iota(jnp.int32, (faces, pad), 0)

    def onehot(slot):
        index = lax.shift_right_logical(rows_ref[slot : slot + 1, :], CX.bit_length() - 1)
        return jnp.where(face_cell == index, 1.0, 0.0).astype(jnp.bfloat16)

    for slot in range(1, SLOTS, 2):
        hot_ref[slot // 2] = onehot(slot)
    for c in range(width // LANES):
        load(c).wait()
    for g in range(layers // per):
        total = jnp.zeros((2 * K, 2 * LANES), jnp.float32)
        sig_row = jnp.zeros((1, 2 * LANES), jnp.float32)
        for i in range(per):
            z = g * per + i
            total = total + dot_nn(split(layer(z)), sel_ref[i])
            sig_row = sig_row + placed[i][z : z + 1]
        high, low = halves(sig_row)
        sig_rows = jnp.concatenate(
            [jnp.broadcast_to(high, (SUB, 2 * LANES)), jnp.broadcast_to(low, (SUB, 2 * LANES))], axis=0
        )
        stacked = jnp.concatenate([total, sig_rows], axis=0).astype(jnp.bfloat16)
        for f in range(2):
            lhs_ref[f, :, g * LANES : (g + 1) * LANES] = stacked[:, f * LANES : (f + 1) * LANES]

    lay_out[:K] = layer(0)
    lay_out[K:] = jnp.broadcast_to(sigma[:1], (SUB, width))
    sig_out[...] = jnp.broadcast_to(sigma[layers - 1 :], (SUB, width))

    beside = jnp.minimum(me, REACH) + jnp.minimum(n_sub - 1 - me, REACH)
    pl.semaphore_wait(barrier, beside + groups - 1)

    def down():
        return pltpu.make_async_remote_copy(
            src_ref=lay_out, dst_ref=lay_in, send_sem=lay_send.at[0], recv_sem=lay_recv.at[0],
            device_id={"coarse": level - 1}, device_id_type=MESH,
        )

    def up():
        return pltpu.make_async_remote_copy(
            src_ref=sig_out, dst_ref=sig_in, send_sem=lay_send.at[1], recv_sem=lay_recv.at[1],
            device_id={"coarse": level + 1}, device_id_type=MESH,
        )

    @pl.when(level > 0)
    def _():
        down().start()

    @pl.when(level < groups - 1)
    def _():
        up().start()

    def picked_copy(slot):
        mirror = SLOTS - 1 - slot
        return pltpu.make_async_remote_copy(
            src_ref=out_ref.at[slot], dst_ref=in_ref.at[mirror // 2],
            send_sem=send_sem.at[slot // 2], recv_sem=recv_sem.at[mirror // 2],
            device_id={"sub": me + offset_of(slot)}, device_id_type=MESH,
        )

    def sigma_copy(slot):
        mirror = SLOTS - 1 - slot
        return pltpu.make_async_remote_copy(
            src_ref=psig_out.at[slot], dst_ref=psig_in.at[mirror],
            send_sem=psig_send.at[slot], recv_sem=psig_recv.at[mirror],
            device_id={"sub": me + offset_of(slot)}, device_id_type=MESH,
        )

    for batch in ((1, 7), (3, 5), (0, 2, 4, 6)):
        for slot in batch:
            hot = hot_ref[slot // 2] if slot % 2 else onehot(slot)
            picked = dot_nn(lhs_ref[0 if slot < REACH else 1], hot)
            out_ref[slot] = picked[:K] + picked[K : 2 * K]
            psig_out[slot] = picked[2 * K : 2 * K + SUB] + picked[2 * K + SUB :]
        for slot in batch:
            @pl.when(reachable(slot))
            def _():
                if slot % 2:
                    picked_copy(slot).start()
                sigma_copy(slot).start()

    def some_layers(step, gram):
        start = step * per
        cells = [layer(start + i) for i in range(per)]
        cells.append(layer(min(start + per, layers - 1)))
        lefts, rights = [], []
        for i in range(per):
            z = start + i
            here = cells[i]
            applied = (
                coef_ref[0, z : z + 1, :] * here
                - coef_ref[1, z : z + 1, :] * pltpu.roll(here, width - 1, 1)
                - coef_ref[2, z : z + 1, :] * pltpu.roll(here, width - CX, 1)
                - coef_ref[3, z : z + 1, :] * cells[i + 1]
            )
            lefts.append(split(here))
            rights.append(split(applied))
        return gram + dot_nt(jnp.concatenate(lefts, axis=1), jnp.concatenate(rights, axis=1))

    gram = jnp.zeros((2 * K, 2 * K), jnp.float32)
    for step in range(layers // per):
        gram = some_layers(step, gram)
    half = quad(gram)
    own = half + half.T

    @pl.when(level < groups - 1)
    def _():
        down().wait_recv()

    @pl.when(level > 0)
    def _():
        up().wait_recv()

    for slot in range(SLOTS):
        @pl.when(reachable(slot))
        def _():
            sigma_copy(SLOTS - 1 - slot).wait_recv()

    has_above = level < groups - 1
    has_below = level > 0
    top = layer(layers - 1)
    bottom = layer(0)
    above = jnp.where(has_above, lay_in[:K], 0.0)
    upper = jnp.where(has_above, harmonic(sigma[layers - 1 :], lay_in[K : K + 1]), 0.0)
    lower = jnp.where(has_below, harmonic(sigma[:1], sig_in[:1]), 0.0)
    top_weighted = split(top * upper)
    upper_block = -quad(dot_nt(top_weighted, split(above)))
    spot = lax.broadcasted_iota(jnp.int32, (1, pad), 1)
    lefts = [top_weighted, split(bottom * lower)]
    rights = [split(top), split(bottom)]
    for slot in range(SLOTS):
        live = jnp.logical_and(spot < cnt_ref[0, 0, slot], reachable(slot))
        weight = jnp.where(live, harmonic(psig_out[slot, :1], psig_in[slot, :1]), 0.0)
        rows = out_ref[slot]
        lefts.append(split(rows * weight))
        rights.append(split(rows))
        if slot % 2 == 0:
            wgt_ref[slot // 2] = lefts[-1]
    own = own + quad(dot_nt(jnp.concatenate(lefts, axis=1), jnp.concatenate(rights, axis=1)))

    band = jnp.concatenate([own, upper_block], axis=1)
    own_band[...] = band

    def band_copy(step):
        return pltpu.make_async_remote_copy(
            src_ref=own_band, dst_ref=bands_ref.at[level],
            send_sem=band_send.at[step], recv_sem=band_recv.at[level],
            device_id={"coarse": lax.rem(level + step, groups)}, device_id_type=MESH,
        )

    for step in range(1, groups):
        band_copy(step).start()
    bands_ref[level] = band

    def ret_copy(slot):
        return pltpu.make_async_remote_copy(
            src_ref=ret_out.at[slot], dst_ref=ret_in.at[SLOTS - 1 - slot],
            send_sem=ret_send.at[slot], recv_sem=ret_recv.at[SLOTS - 1 - slot],
            device_id={"sub": me + offset_of(slot)}, device_id_type=MESH,
        )

    def ret_arrival(slot):
        return pltpu.make_async_remote_copy(
            src_ref=ret_out.at[SLOTS - 1 - slot], dst_ref=ret_in.at[slot],
            send_sem=ret_send.at[SLOTS - 1 - slot], recv_sem=ret_recv.at[slot],
            device_id={"sub": me + offset_of(slot)}, device_id_type=MESH,
        )

    for slot in range(0, SLOTS, 2):
        @pl.when(reachable(slot))
        def _():
            picked_copy(SLOTS - 1 - slot).wait_recv()

    wide = jnp.zeros((K, LANES - K), jnp.float32)
    for slot in range(0, SLOTS, 2):
        partner = jnp.where(reachable(slot), in_ref[slot // 2], 0.0)
        block = -quad(dot_nt(wgt_ref[slot // 2], split(partner)))
        blk_ref[slot] = block
        ret_out[slot] = jnp.concatenate([block.T, wide], axis=1)
    for slot in range(0, SLOTS, 2):
        @pl.when(reachable(slot))
        def _():
            ret_copy(slot).start()

    for slot in range(SLOTS):
        if slot % 2:
            @pl.when(reachable(slot))
            def _():
                ret_arrival(slot).wait_recv()

            blk_ref[slot] = jnp.where(reachable(slot), ret_in[slot, :, :K], 0.0)
    for pair in range(SLOTS // 2):
        lat_ref[:, pair * 2 * K : (pair + 1) * 2 * K] = jnp.concatenate(
            [blk_ref[2 * pair], blk_ref[2 * pair + 1]], axis=1
        )
    for step in range(1, groups):
        source = lax.rem(level + groups - step, groups)
        pltpu.make_async_remote_copy(
            src_ref=own_band, dst_ref=bands_ref.at[source],
            send_sem=band_send.at[step], recv_sem=band_recv.at[source],
            device_id={"coarse": source}, device_id_type=MESH,
        ).wait_recv()
    for step in range(1, groups):
        band_copy(step).wait_send()
    for slot in range(SLOTS):
        @pl.when(reachable(slot))
        def _():
            sigma_copy(slot).wait_send()
            if slot % 2:
                picked_copy(slot).wait_send()
            else:
                ret_copy(slot).wait_send()

    @pl.when(level > 0)
    def _():
        down().wait_send()

    @pl.when(level < groups - 1)
    def _():
        up().wait_send()


def spread(x, at):
    return jnp.broadcast_to(x[at : at + 1, :], x.shape)


def column(x, at):
    return jnp.broadcast_to(x[:, at : at + 1], (x.shape[0], LANES))


def eliminate(left, right):
    left, right = list(left), list(right)
    below = lax.broadcasted_iota(jnp.int32, (SUB, LANES), 0)
    for p in range(K // SUB):
        cols = [[column(left[g], p * SUB + j) for j in range(SUB)] for g in range(p, K // SUB)]
        head = cols[0]
        a, b = left[p], right[p]
        inverses, above, rows_a, rows_b, roots = [], [], [], [], []
        for j in range(0, SUB, 2):
            first, cross, second = spread(head[j], j), spread(head[j + 1], j), spread(head[j + 1], j + 1)
            inverse_1 = 1.0 / first
            inverse_2 = first * (1.0 / (first * second - cross * cross))
            ratio = cross * inverse_1
            scale_1 = jnp.where(below > j, head[j], 0.0) * inverse_1
            scale_2 = jnp.where(below > j + 1, head[j + 1] - scale_1 * cross, 0.0) * inverse_2

            def pair(x):
                top = spread(x, j)
                return top, spread(x, j + 1) - ratio * top

            entries_1, entries_2 = {j + 1: cross}, {}
            for k in range(j + 2, SUB):
                entries_1[k], entries_2[k] = pair(head[k])
                head[k] = (head[k] - scale_1 * entries_1[k]) - scale_2 * entries_2[k]
            inverses += [inverse_1, inverse_2]
            roots += [lax.rsqrt(first), lax.rsqrt(second - ratio * cross)]
            above += [entries_1, entries_2]
            top_a, next_a = pair(a)
            top_b, next_b = pair(b)
            a = (a - scale_1 * top_a) - scale_2 * next_a
            b = (b - scale_1 * top_b) - scale_2 * next_b
            rows_a += [top_a, next_a]
            rows_b += [top_b, next_b]
        left[p], right[p] = a, b
        for g in range(p + 1, K // SUB):
            tail = cols[g - p]
            la, lb = left[g], right[g]
            for j in range(SUB):
                scale = tail[j] * inverses[j]
                for k in range(j + 1, SUB):
                    tail[k] = tail[k] - scale * above[j][k]
                la = la - scale * rows_a[j]
                lb = lb - scale * rows_b[j]
            left[g], right[g] = la, lb
        for j in range(SUB):
            left[p] = jnp.where(below == j, left[p] * roots[j], left[p])
            right[p] = jnp.where(below == j, right[p] * roots[j], right[p])
    return left, right


def thirds(x):
    high, rest = halves(x)
    middle, low = halves(rest)
    return high, middle, low


def exact_tn(left, right):
    a, b, c = thirds(left)
    d, e, f = thirds(right)
    return lax.dot_general(
        jnp.concatenate([a, a, b, b, a, c], axis=0).astype(jnp.bfloat16),
        jnp.concatenate([d, e, d, e, f, d], axis=0).astype(jnp.bfloat16),
        (((0,), (0,)), ((), ())), preferred_element_type=jnp.float32,
    )


def factor_kernel(
    groups, bands_ref, lat_ref, factor_ref, panel_ref, low_ref, inv_ref, turn_ref, schur_ref, last_ref, scaled_ref, fit_ref
):
    level = lax.axis_index("coarse")
    row = lax.broadcasted_iota(jnp.int32, (K, LANES), 0)
    lane = lax.broadcasted_iota(jnp.int32, (K, LANES), 1)
    eye = jnp.where(row == lane, 1.0, 0.0)
    fit = []
    for k in range(groups):
        diagonal = jnp.where(row == lane, bands_ref[k], 0.0)
        fit.append((jnp.sum(diagonal, axis=0, keepdims=True)[:, :K], jnp.sum(diagonal, axis=1, keepdims=True)))
    for k in range(groups):
        after = fit[k + 1][0] if k + 1 < groups else jnp.ones((1, K), jnp.float32)
        along = jnp.concatenate([fit[k][0], after], axis=1)
        shrink = lax.rsqrt(along)
        scaled_ref[k] = bands_ref[k] * shrink * lax.rsqrt(fit[k][1])
        fit_ref[k, :1] = along * shrink
        fit_ref[k, 1:2] = shrink
    schur_ref[...] = jnp.zeros_like(schur_ref)
    last_ref[...] = jnp.zeros_like(last_ref)
    low_ref[0] = jnp.zeros_like(low_ref[0])
    inv_ref[0] = jnp.zeros_like(inv_ref[0])
    turn_ref[0] = jnp.zeros_like(turn_ref[0])

    def panel_block(k, before):
        right = jnp.where(level == k, lat_ref[...], 0.0) - exact_tn(turn_ref[before], last_ref[...])
        return exact_tn(inv_ref[jnp.maximum(k, 0)], right)

    def one_block(k, carry):
        done = jnp.maximum(k - 1, 0)
        last = panel_block(k - 1, jnp.maximum(k - 2, 0))
        start = scaled_ref[k] - schur_ref[...]
        tiles = [start[g * SUB : (g + 1) * SUB] for g in range(K // SUB)]
        ones = [eye[g * SUB : (g + 1) * SUB] for g in range(K // SUB)]
        left, right = eliminate(tiles, ones)
        left = jnp.concatenate(left, axis=0)
        right = jnp.concatenate(right, axis=0)
        left = jnp.where(lane >= row, left, 0.0)
        turn = left[:, K:]
        real_turn = (left * fit_ref[k, :1])[:, K:]
        last_ref[...] = last
        panel_ref[0, 0, pl.ds(pl.multiple_of(done * K, K), K), :] = last
        low_ref[k] = (left * fit_ref[k, :1]).T
        inv_ref[k] = (right * fit_ref[k, 1:2]).T[:K]
        turn_ref[k] = real_turn
        schur_ref[:, :K] = exact_tn(turn, turn)
        return carry

    factor_ref[0] = jnp.zeros_like(factor_ref[0])
    lax.fori_loop(0, groups, one_block, 0)
    panel_ref[0, 0, (groups - 1) * K :, :] = panel_block(groups - 1, groups - 2)
    for k in range(groups):
        factor_ref[0, k * K : (k + 1) * K, k * K : (k + 1) * K] = low_ref[k, :K]
        if k + 1 < groups:
            factor_ref[0, (k + 1) * K : (k + 2) * K, k * K : (k + 1) * K] = low_ref[k, K:]


def body(n_sub, groups, deflation, conductivity, storage, interface_rows, interface_counts):
    layers, width = deflation.shape[2], deflation.shape[3]
    pad = interface_rows.shape[3]
    faces = width // CX * layers
    f32 = jnp.float32
    vmem = pl.BlockSpec(memory_space=pltpu.VMEM)
    dma = pltpu.SemaphoreType.DMA
    bands, lateral = pl.pallas_call(
        functools.partial(couple_kernel, n_sub, groups, layers, width),
        out_shape=(
            jax.ShapeDtypeStruct((groups, K, 2 * K), f32),
            jax.ShapeDtypeStruct((K, SLOTS * K), f32),
        ),
        in_specs=[pl.BlockSpec(memory_space=pltpu.HBM)] * 5,
        out_specs=(vmem, vmem),
        scratch_shapes=[
            pltpu.VMEM((width // LANES * K * layers, LANES), f32),
            dma((width // LANES,)),
            pltpu.VMEM((layers, width), f32),
            pltpu.VMEM((layers, width), f32),
            pltpu.VMEM((SLOTS, pad), jnp.int32),
            pltpu.SMEM((1, 1, SLOTS), jnp.int32),
            dma((4,)),
            pltpu.VMEM((LANES * CX // width, width, 2 * LANES), jnp.bfloat16),
            pltpu.VMEM((2, 2 * K + 2 * SUB, faces), jnp.bfloat16),
            pltpu.VMEM((4, layers, width), f32),
            pltpu.VMEM((SLOTS, K, pad), f32),
            pltpu.VMEM((REACH, K, pad), f32),
            pltpu.VMEM((SLOTS, SUB, pad), f32),
            pltpu.VMEM((SLOTS, SUB, pad), f32),
            pltpu.VMEM((K + SUB, width), f32),
            pltpu.VMEM((K + SUB, width), f32),
            pltpu.VMEM((SUB, width), f32),
            pltpu.VMEM((SUB, width), f32),
            pltpu.VMEM((SLOTS, K, LANES), f32),
            pltpu.VMEM((SLOTS, K, LANES), f32),
            pltpu.VMEM((SLOTS, K, K), f32),
            pltpu.VMEM((REACH, 2 * K, pad), jnp.bfloat16),
            pltpu.VMEM((REACH, faces, pad), jnp.bfloat16),
            pltpu.VMEM((K, 2 * K), f32),
            dma((REACH,)), dma((REACH,)), dma((SLOTS,)), dma((SLOTS,)), dma((2,)), dma((2,)),
            dma((SLOTS,)), dma((SLOTS,)), dma((groups,)), dma((groups,)),
        ],
        compiler_params=pltpu.CompilerParams(
            collective_id=0, has_side_effects=True, vmem_limit_bytes=40 * 1024 * 1024
        ),
        name="couple",
    )(
        *(
            pltpu.with_memory_space_constraint(x, pltpu.HBM)
            for x in (
                deflation.reshape(K * layers, width), conductivity[0], storage[0],
                interface_rows[0, 0], interface_counts,
            )
        )
    )
    return pl.pallas_call(
        functools.partial(factor_kernel, groups),
        out_shape=(
            jax.ShapeDtypeStruct((1, groups * K, groups * K), f32),
            jax.ShapeDtypeStruct((1, 1, groups * K, SLOTS * K), f32),
        ),
        in_specs=[vmem, vmem],
        out_specs=(vmem, vmem),
        scratch_shapes=[
            pltpu.VMEM((groups, 2 * K, K), f32),
            pltpu.VMEM((groups, K, K), f32),
            pltpu.VMEM((groups, K, K), f32),
            pltpu.VMEM((K, LANES), f32),
            pltpu.VMEM((K, SLOTS * K), f32),
            pltpu.VMEM((groups, K, LANES), f32),
            pltpu.VMEM((groups, SUB, LANES), f32),
        ],
        compiler_params=pltpu.CompilerParams(vmem_limit_bytes=40 * 1024 * 1024),
        name="factor",
    )(bands, lateral)


def solution(mesh):
    placed = (
        P("sub", None, "coarse", None),
        P("sub", "coarse", None),
        P("sub", "coarse", None),
        P("sub", "coarse", None, None),
        P("sub", "coarse", None),
    )
    return jax.shard_map(
        functools.partial(body, mesh.shape["sub"], mesh.shape["coarse"]),
        mesh=mesh,
        in_specs=placed,
        out_specs=(P("sub", None, None), P("sub", "coarse", None, None)),
        check_vma=False,
    )
```

```python
import functools

import jax
import jax.numpy as jnp
from jax import lax
from jax.experimental import pallas as pl
from jax.experimental.pallas import tpu as pltpu
from jax.sharding import PartitionSpec as P

K = 64
CX = 16
REACH = 4
LANES = 128
SUB = 8
SLOTS = 2 * REACH
MESH = pl.DeviceIdType.MESH


def harmonic(first, second):
    return 2.0 * first * second / (first + second)


def offset_of(slot):
    return slot - REACH if slot < REACH else slot - REACH + 1


def halves(x):
    high = x.astype(jnp.bfloat16).astype(jnp.float32)
    return high, x - high


def split(x):
    return jnp.concatenate(halves(x), axis=0).astype(jnp.bfloat16)


def dot_nn(left, right):
    return lax.dot_general(left, right, (((1,), (0,)), ((), ())), preferred_element_type=jnp.float32)


def dot_nt(left, right):
    return lax.dot_general(left, right, (((1,), (1,)), ((), ())), preferred_element_type=jnp.float32)


def quad(g, at=0):
    return (g[:K, at : at + K] + g[K:, at : at + K]) + (g[:K, at + K : at + 2 * K] + g[K:, at + K : at + 2 * K])


def spread(x, at):
    return jnp.broadcast_to(x[at : at + 1, :], x.shape)


def column(x, at):
    return jnp.broadcast_to(x[:, at : at + 1], (x.shape[0], LANES))


def eliminate(left, right):
    left, right = list(left), list(right)
    below = lax.broadcasted_iota(jnp.int32, (SUB, LANES), 0)
    for p in range(K // SUB):
        cols = [[column(left[g], p * SUB + j) for j in range(SUB)] for g in range(p, K // SUB)]
        head = cols[0]
        a, b = left[p], right[p]
        inverses, above, rows_a, rows_b, roots = [], [], [], [], []
        for j in range(0, SUB, 2):
            first, cross, second = spread(head[j], j), spread(head[j + 1], j), spread(head[j + 1], j + 1)
            inverse_1 = 1.0 / first
            inverse_2 = first * (1.0 / (first * second - cross * cross))
            ratio = cross * inverse_1
            scale_1 = jnp.where(below > j, head[j], 0.0) * inverse_1
            scale_2 = jnp.where(below > j + 1, head[j + 1] - scale_1 * cross, 0.0) * inverse_2

            def pair(x):
                top = spread(x, j)
                return top, spread(x, j + 1) - ratio * top

            entries_1, entries_2 = {j + 1: cross}, {}
            for k in range(j + 2, SUB):
                entries_1[k], entries_2[k] = pair(head[k])
                head[k] = (head[k] - scale_1 * entries_1[k]) - scale_2 * entries_2[k]
            inverses += [inverse_1, inverse_2]
            roots += [lax.rsqrt(first), lax.rsqrt(second - ratio * cross)]
            above += [entries_1, entries_2]
            top_a, next_a = pair(a)
            top_b, next_b = pair(b)
            a = (a - scale_1 * top_a) - scale_2 * next_a
            b = (b - scale_1 * top_b) - scale_2 * next_b
            rows_a += [top_a, next_a]
            rows_b += [top_b, next_b]
        left[p], right[p] = a, b
        for g in range(p + 1, K // SUB):
            tail = cols[g - p]
            la, lb = left[g], right[g]
            for j in range(SUB):
                scale = tail[j] * inverses[j]
                for k in range(j + 1, SUB):
                    tail[k] = tail[k] - scale * above[j][k]
                la = la - scale * rows_a[j]
                lb = lb - scale * rows_b[j]
            left[g], right[g] = la, lb
        for j in range(SUB):
            left[p] = jnp.where(below == j, left[p] * roots[j], left[p])
            right[p] = jnp.where(below == j, right[p] * roots[j], right[p])
    return left, right


def thirds(x):
    high, rest = halves(x)
    middle, low = halves(rest)
    return high, middle, low


def exact_tn(left, right):
    a, b, c = thirds(left)
    d, e, f = thirds(right)
    return lax.dot_general(
        jnp.concatenate([a, a, b, b, a, c], axis=0).astype(jnp.bfloat16),
        jnp.concatenate([d, e, d, e, f, d], axis=0).astype(jnp.bfloat16),
        (((0,), (0,)), ((), ())), preferred_element_type=jnp.float32,
    )


def couple_kernel(
    n_sub, groups, layers, width,
    z_hbm, sig_hbm, sto_hbm, rows_hbm, cnt_hbm,
    factor_ref, panel_ref,
    bands_ref, lat_ref, low_ref, inv_ref, turn_ref, schur_ref, last_ref, scaled_ref, fit_ref,
    z_ref, load_sem, sig_ref, sto_ref, rows_ref, cnt_ref, small_sem, sel_ref, lhs_ref, coef_ref, out_ref, in_ref, psig_out, psig_in, lay_out, lay_in, sig_out, sig_in,
    ret_out, ret_in, blk_ref, wgt_ref, hot_ref, own_band,
    send_sem, recv_sem, psig_send, psig_recv, lay_send, lay_recv, ret_send, ret_recv, band_send, band_recv,
):
    me = lax.axis_index("sub")
    level = lax.axis_index("coarse")
    cy = width // CX
    per = LANES // cy
    pad = rows_ref.shape[1]
    faces = cy * layers

    def load(c):
        return pltpu.make_async_copy(
            z_hbm.at[:, pl.ds(c * LANES, LANES)], z_ref.at[pl.ds(c * K * layers, K * layers)], load_sem.at[c]
        )

    small = [
        pltpu.make_async_copy(src, dst, small_sem.at[i])
        for i, (src, dst) in enumerate(
            ((sig_hbm, sig_ref), (rows_hbm, rows_ref), (sto_hbm, sto_ref), (cnt_hbm, cnt_ref))
        )
    ]
    for copy in small:
        copy.start()
    for c in range(width // LANES):
        load(c).start()

    def layer(z):
        return jnp.concatenate(
            [z_ref[pl.ds(c * K * layers + z, K, stride=layers), :] for c in range(width // LANES)], axis=1
        )

    def reachable(slot):
        other = me + offset_of(slot)
        return jnp.logical_and(other >= 0, other < n_sub)

    barrier = pltpu.get_barrier_semaphore()
    for slot in range(SLOTS):
        @pl.when(reachable(slot))
        def _():
            pl.semaphore_signal(barrier, inc=1, device_id={"sub": me + offset_of(slot)}, device_id_type=MESH)
    for step in range(1, groups):
        pl.semaphore_signal(
            barrier, inc=1, device_id={"coarse": lax.rem(level + step, groups)}, device_id_type=MESH
        )

    row = lax.broadcasted_iota(jnp.int32, (width, 2 * LANES), 0)
    lane = lax.broadcasted_iota(jnp.int32, (width, 2 * LANES), 1)
    cell = (lane % cy) * CX + jnp.where(lane >= LANES, CX - 1, 0)
    hit = row == cell
    part = (lane % LANES) // cy
    for i in range(per):
        sel_ref[i] = jnp.where(jnp.logical_and(hit, part == i), 1.0, 0.0).astype(jnp.bfloat16)

    for copy in small:
        copy.wait()
    sigma = sig_ref[...]
    sigma_split = split(sigma)
    placed = []
    for i in range(per):
        t = dot_nn(sigma_split, sel_ref[i])
        placed.append(t[:layers] + t[layers:])
    position = lax.broadcasted_iota(jnp.int32, (layers, width), 1)
    depth = lax.broadcasted_iota(jnp.int32, (layers, width), 0)
    wx = jnp.where(position % CX == CX - 1, 0.0, harmonic(sigma, pltpu.roll(sigma, width - 1, 1)))
    wy = jnp.where(position >= width - CX, 0.0, harmonic(sigma, pltpu.roll(sigma, width - CX, 1)))
    wz = jnp.where(depth == layers - 1, 0.0, harmonic(sigma, pltpu.roll(sigma, layers - 1, 0)))
    coef_ref[0] = 0.5 * (
        sto_ref[...] + (wx + pltpu.roll(wx, 1, 1)) + (wy + pltpu.roll(wy, CX, 1)) + (wz + pltpu.roll(wz, 1, 0))
    )
    coef_ref[1] = wx
    coef_ref[2] = wy
    coef_ref[3] = wz

    face_cell = lax.broadcasted_iota(jnp.int32, (faces, pad), 0)

    def onehot(slot):
        index = lax.shift_right_logical(rows_ref[slot : slot + 1, :], CX.bit_length() - 1)
        return jnp.where(face_cell == index, 1.0, 0.0).astype(jnp.bfloat16)

    for slot in range(1, SLOTS, 2):
        hot_ref[slot // 2] = onehot(slot)
    for c in range(width // LANES):
        load(c).wait()
    for g in range(layers // per):
        total = jnp.zeros((2 * K, 2 * LANES), jnp.float32)
        sig_row = jnp.zeros((1, 2 * LANES), jnp.float32)
        for i in range(per):
            z = g * per + i
            total = total + dot_nn(split(layer(z)), sel_ref[i])
            sig_row = sig_row + placed[i][z : z + 1]
        high, low = halves(sig_row)
        sig_rows = jnp.concatenate(
            [jnp.broadcast_to(high, (SUB, 2 * LANES)), jnp.broadcast_to(low, (SUB, 2 * LANES))], axis=0
        )
        stacked = jnp.concatenate([total, sig_rows], axis=0).astype(jnp.bfloat16)
        for f in range(2):
            lhs_ref[f, :, g * LANES : (g + 1) * LANES] = stacked[:, f * LANES : (f + 1) * LANES]

    lay_out[:K] = layer(0)
    lay_out[K:] = jnp.broadcast_to(sigma[:1], (SUB, width))
    sig_out[...] = jnp.broadcast_to(sigma[layers - 1 :], (SUB, width))

    beside = jnp.minimum(me, REACH) + jnp.minimum(n_sub - 1 - me, REACH)
    pl.semaphore_wait(barrier, beside + groups - 1)

    def down():
        return pltpu.make_async_remote_copy(
            src_ref=lay_out, dst_ref=lay_in, send_sem=lay_send.at[0], recv_sem=lay_recv.at[0],
            device_id={"coarse": level - 1}, device_id_type=MESH,
        )

    def up():
        return pltpu.make_async_remote_copy(
            src_ref=sig_out, dst_ref=sig_in, send_sem=lay_send.at[1], recv_sem=lay_recv.at[1],
            device_id={"coarse": level + 1}, device_id_type=MESH,
        )

    @pl.when(level > 0)
    def _():
        down().start()

    @pl.when(level < groups - 1)
    def _():
        up().start()

    def picked_copy(slot):
        mirror = SLOTS - 1 - slot
        return pltpu.make_async_remote_copy(
            src_ref=out_ref.at[slot], dst_ref=in_ref.at[mirror // 2],
            send_sem=send_sem.at[slot // 2], recv_sem=recv_sem.at[mirror // 2],
            device_id={"sub": me + offset_of(slot)}, device_id_type=MESH,
        )

    def sigma_copy(slot):
        mirror = SLOTS - 1 - slot
        return pltpu.make_async_remote_copy(
            src_ref=psig_out.at[slot], dst_ref=psig_in.at[mirror],
            send_sem=psig_send.at[slot], recv_sem=psig_recv.at[mirror],
            device_id={"sub": me + offset_of(slot)}, device_id_type=MESH,
        )

    for batch in ((1, 7), (3, 5), (0, 2, 4, 6)):
        for slot in batch:
            hot = hot_ref[slot // 2] if slot % 2 else onehot(slot)
            picked = dot_nn(lhs_ref[0 if slot < REACH else 1], hot)
            out_ref[slot] = picked[:K] + picked[K : 2 * K]
            psig_out[slot] = picked[2 * K : 2 * K + SUB] + picked[2 * K + SUB :]
        for slot in batch:
            @pl.when(reachable(slot))
            def _():
                if slot % 2:
                    picked_copy(slot).start()
                sigma_copy(slot).start()

    def some_layers(step, gram):
        start = step * per
        cells = [layer(start + i) for i in range(per)]
        cells.append(layer(jnp.minimum(start + per, layers - 1)))
        lefts, rights = [], []
        for i in range(per):
            z = start + i
            here = cells[i]
            applied = (
                coef_ref[0, pl.ds(z, 1), :] * here
                - coef_ref[1, pl.ds(z, 1), :] * pltpu.roll(here, width - 1, 1)
                - coef_ref[2, pl.ds(z, 1), :] * pltpu.roll(here, width - CX, 1)
                - coef_ref[3, pl.ds(z, 1), :] * cells[i + 1]
            )
            lefts.append(split(here))
            rights.append(split(applied))
        return gram + dot_nt(jnp.concatenate(lefts, axis=1), jnp.concatenate(rights, axis=1))

    gram = lax.fori_loop(0, layers // per, some_layers, jnp.zeros((2 * K, 2 * K), jnp.float32))
    half = quad(gram)
    own = half + half.T

    @pl.when(level < groups - 1)
    def _():
        down().wait_recv()

    @pl.when(level > 0)
    def _():
        up().wait_recv()

    for slot in range(SLOTS):
        @pl.when(reachable(slot))
        def _():
            sigma_copy(SLOTS - 1 - slot).wait_recv()

    has_above = level < groups - 1
    has_below = level > 0
    top = layer(layers - 1)
    bottom = layer(0)
    above = jnp.where(has_above, lay_in[:K], 0.0)
    upper = jnp.where(has_above, harmonic(sigma[layers - 1 :], lay_in[K : K + 1]), 0.0)
    lower = jnp.where(has_below, harmonic(sigma[:1], sig_in[:1]), 0.0)
    top_weighted = split(top * upper)
    upper_block = -quad(dot_nt(top_weighted, split(above)))
    spot = lax.broadcasted_iota(jnp.int32, (1, pad), 1)
    lefts = [top_weighted, split(bottom * lower)]
    rights = [split(top), split(bottom)]
    for slot in range(SLOTS):
        live = jnp.logical_and(spot < cnt_ref[0, 0, slot], reachable(slot))
        weight = jnp.where(live, harmonic(psig_out[slot, :1], psig_in[slot, :1]), 0.0)
        rows = out_ref[slot]
        lefts.append(split(rows * weight))
        rights.append(split(rows))
        if slot % 2 == 0:
            wgt_ref[slot // 2] = lefts[-1]
    own = own + quad(dot_nt(jnp.concatenate(lefts, axis=1), jnp.concatenate(rights, axis=1)))

    band = jnp.concatenate([own, upper_block], axis=1)
    own_band[...] = band

    def band_copy(step):
        return pltpu.make_async_remote_copy(
            src_ref=own_band, dst_ref=bands_ref.at[level],
            send_sem=band_send.at[step], recv_sem=band_recv.at[level],
            device_id={"coarse": lax.rem(level + step, groups)}, device_id_type=MESH,
        )

    for step in range(1, groups):
        band_copy(step).start()
    bands_ref[level] = band

    def ret_copy(slot):
        return pltpu.make_async_remote_copy(
            src_ref=ret_out.at[slot], dst_ref=ret_in.at[SLOTS - 1 - slot],
            send_sem=ret_send.at[slot], recv_sem=ret_recv.at[SLOTS - 1 - slot],
            device_id={"sub": me + offset_of(slot)}, device_id_type=MESH,
        )

    def ret_arrival(slot):
        return pltpu.make_async_remote_copy(
            src_ref=ret_out.at[SLOTS - 1 - slot], dst_ref=ret_in.at[slot],
            send_sem=ret_send.at[SLOTS - 1 - slot], recv_sem=ret_recv.at[slot],
            device_id={"sub": me + offset_of(slot)}, device_id_type=MESH,
        )

    for slot in range(0, SLOTS, 2):
        @pl.when(reachable(slot))
        def _():
            picked_copy(SLOTS - 1 - slot).wait_recv()

    wide = jnp.zeros((K, LANES - K), jnp.float32)
    for slot in range(0, SLOTS, 2):
        partner = jnp.where(reachable(slot), in_ref[slot // 2], 0.0)
        block = -quad(dot_nt(wgt_ref[slot // 2], split(partner)))
        blk_ref[slot] = block
        ret_out[slot] = jnp.concatenate([block.T, wide], axis=1)
    for slot in range(0, SLOTS, 2):
        @pl.when(reachable(slot))
        def _():
            ret_copy(slot).start()

    for step in range(1, groups):
        source = lax.rem(level + groups - step, groups)
        pltpu.make_async_remote_copy(
            src_ref=own_band, dst_ref=bands_ref.at[source],
            send_sem=band_send.at[step], recv_sem=band_recv.at[source],
            device_id={"coarse": source}, device_id_type=MESH,
        ).wait_recv()
    row_id = lax.broadcasted_iota(jnp.int32, (K, LANES), 0)
    lane_id = lax.broadcasted_iota(jnp.int32, (K, LANES), 1)
    eye = jnp.where(row_id == lane_id, 1.0, 0.0)
    fit = []
    for k in range(groups):
        diagonal = jnp.where(row_id == lane_id, bands_ref[k], 0.0)
        fit.append((jnp.sum(diagonal, axis=0, keepdims=True)[:, :K], jnp.sum(diagonal, axis=1, keepdims=True)))
    for k in range(groups):
        after = fit[k + 1][0] if k + 1 < groups else jnp.ones((1, K), jnp.float32)
        along = jnp.concatenate([fit[k][0], after], axis=1)
        shrink = lax.rsqrt(along)
        scaled_ref[k] = bands_ref[k] * shrink * lax.rsqrt(fit[k][1])
        fit_ref[k, :1] = along * shrink
        fit_ref[k, 1:2] = shrink
    schur_ref[...] = jnp.zeros_like(schur_ref)
    last_ref[...] = jnp.zeros_like(last_ref)

    def panel_block(k, before):
        right = jnp.where(level == k, lat_ref[...], 0.0) - exact_tn(turn_ref[before], last_ref[...])
        return exact_tn(inv_ref[k], right)

    def one_block(k, carry):
        last = panel_block(k - 1, jnp.maximum(k - 2, 0)) if carry is not None else None
        start = scaled_ref[k] - schur_ref[...]
        tiles = [start[g * SUB : (g + 1) * SUB] for g in range(K // SUB)]
        ones = [eye[g * SUB : (g + 1) * SUB] for g in range(K // SUB)]
        left, right = eliminate(tiles, ones)
        left = jnp.concatenate(left, axis=0)
        right = jnp.concatenate(right, axis=0)
        left = jnp.where(lane_id >= row_id, left, 0.0)
        turn = left[:, K:]
        real_turn = (left * fit_ref[k, :1])[:, K:]
        if last is not None:
            last_ref[...] = last
            panel_ref[0, 0, pl.ds(pl.multiple_of((k - 1) * K, K), K), :] = last
        low_ref[k] = (left * fit_ref[k, :1]).T
        inv_ref[k] = (right * fit_ref[k, 1:2]).T[:K]
        turn_ref[k] = real_turn
        schur_ref[:, :K] = exact_tn(turn, turn)
        return carry

    factor_ref[0] = jnp.zeros_like(factor_ref[0])
    one_block(0, None)
    for slot in range(SLOTS):
        if slot % 2:
            @pl.when(reachable(slot))
            def _():
                ret_arrival(slot).wait_recv()

            blk_ref[slot] = jnp.where(reachable(slot), ret_in[slot, :, :K], 0.0)
    for pair in range(SLOTS // 2):
        lat_ref[:, pair * 2 * K : (pair + 1) * 2 * K] = jnp.concatenate(
            [blk_ref[2 * pair], blk_ref[2 * pair + 1]], axis=1
        )
    lax.fori_loop(1, groups, one_block, 0)
    panel_ref[0, 0, (groups - 1) * K :, :] = panel_block(groups - 1, groups - 2)
    for k in range(groups):
        factor_ref[0, k * K : (k + 1) * K, k * K : (k + 1) * K] = low_ref[k, :K]
        if k + 1 < groups:
            factor_ref[0, (k + 1) * K : (k + 2) * K, k * K : (k + 1) * K] = low_ref[k, K:]
    for step in range(1, groups):
        band_copy(step).wait_send()
    for slot in range(SLOTS):
        @pl.when(reachable(slot))
        def _():
            sigma_copy(slot).wait_send()
            if slot % 2:
                picked_copy(slot).wait_send()
            else:
                ret_copy(slot).wait_send()

    @pl.when(level > 0)
    def _():
        down().wait_send()

    @pl.when(level < groups - 1)
    def _():
        up().wait_send()


def body(n_sub, groups, deflation, conductivity, storage, interface_rows, interface_counts):
    layers, width = deflation.shape[2], deflation.shape[3]
    pad = interface_rows.shape[3]
    faces = width // CX * layers
    f32 = jnp.float32
    vmem = pl.BlockSpec(memory_space=pltpu.VMEM)
    dma = pltpu.SemaphoreType.DMA
    return pl.pallas_call(
        functools.partial(couple_kernel, n_sub, groups, layers, width),
        out_shape=(
            jax.ShapeDtypeStruct((1, groups * K, groups * K), f32),
            jax.ShapeDtypeStruct((1, 1, groups * K, SLOTS * K), f32),
        ),
        in_specs=[pl.BlockSpec(memory_space=pltpu.HBM)] * 5,
        out_specs=(vmem, vmem),
        scratch_shapes=[
            pltpu.VMEM((groups, K, 2 * K), f32),
            pltpu.VMEM((K, SLOTS * K), f32),
            pltpu.VMEM((groups, 2 * K, K), f32),
            pltpu.VMEM((groups, K, K), f32),
            pltpu.VMEM((groups, K, K), f32),
            pltpu.VMEM((K, LANES), f32),
            pltpu.VMEM((K, SLOTS * K), f32),
            pltpu.VMEM((groups, K, LANES), f32),
            pltpu.VMEM((groups, SUB, LANES), f32),
            pltpu.VMEM((width // LANES * K * layers, LANES), f32),
            dma((width // LANES,)),
            pltpu.VMEM((layers, width), f32),
            pltpu.VMEM((layers, width), f32),
            pltpu.VMEM((SLOTS, pad), jnp.int32),
            pltpu.SMEM((1, 1, SLOTS), jnp.int32),
            dma((4,)),
            pltpu.VMEM((LANES * CX // width, width, 2 * LANES), jnp.bfloat16),
            pltpu.VMEM((2, 2 * K + 2 * SUB, faces), jnp.bfloat16),
            pltpu.VMEM((4, layers, width), f32),
            pltpu.VMEM((SLOTS, K, pad), f32),
            pltpu.VMEM((REACH, K, pad), f32),
            pltpu.VMEM((SLOTS, SUB, pad), f32),
            pltpu.VMEM((SLOTS, SUB, pad), f32),
            pltpu.VMEM((K + SUB, width), f32),
            pltpu.VMEM((K + SUB, width), f32),
            pltpu.VMEM((SUB, width), f32),
            pltpu.VMEM((SUB, width), f32),
            pltpu.VMEM((SLOTS, K, LANES), f32),
            pltpu.VMEM((SLOTS, K, LANES), f32),
            pltpu.VMEM((SLOTS, K, K), f32),
            pltpu.VMEM((REACH, 2 * K, pad), jnp.bfloat16),
            pltpu.VMEM((REACH, faces, pad), jnp.bfloat16),
            pltpu.VMEM((K, 2 * K), f32),
            dma((REACH,)), dma((REACH,)), dma((SLOTS,)), dma((SLOTS,)), dma((2,)), dma((2,)),
            dma((SLOTS,)), dma((SLOTS,)), dma((groups,)), dma((groups,)),
        ],
        compiler_params=pltpu.CompilerParams(
            collective_id=0, has_side_effects=True, vmem_limit_bytes=40 * 1024 * 1024
        ),
        name="couple",
    )(
        *(
            pltpu.with_memory_space_constraint(x, pltpu.HBM)
            for x in (
                deflation.reshape(K * layers, width), conductivity[0], storage[0],
                interface_rows[0, 0], interface_counts,
            )
        )
    )


def solution(mesh):
    placed = (
        P("sub", None, "coarse", None),
        P("sub", "coarse", None),
        P("sub", "coarse", None),
        P("sub", "coarse", None, None),
        P("sub", "coarse", None),
    )
    return jax.shard_map(
        functools.partial(body, mesh.shape["sub"], mesh.shape["coarse"]),
        mesh=mesh,
        in_specs=placed,
        out_specs=(P("sub", None, None), P("sub", "coarse", None, None)),
        check_vma=False,
    )
```

```python
import functools

import jax
import jax.numpy as jnp
from jax import lax
from jax.experimental import pallas as pl
from jax.experimental.pallas import tpu as pltpu
from jax.sharding import PartitionSpec as P

K = 64
CX = 16
REACH = 4
LANES = 128
SUB = 8
SLOTS = 2 * REACH
MESH = pl.DeviceIdType.MESH


def harmonic(first, second):
    return 2.0 * first * second / (first + second)


def offset_of(slot):
    return slot - REACH if slot < REACH else slot - REACH + 1


def halves(x):
    high = x.astype(jnp.bfloat16).astype(jnp.float32)
    return high, x - high


def split(x):
    return jnp.concatenate(halves(x), axis=0).astype(jnp.bfloat16)


def dot_nn(left, right):
    return lax.dot_general(left, right, (((1,), (0,)), ((), ())), preferred_element_type=jnp.float32)


def dot_nt(left, right):
    return lax.dot_general(left, right, (((1,), (1,)), ((), ())), preferred_element_type=jnp.float32)


def quad(g, at=0):
    return (g[:K, at : at + K] + g[K:, at : at + K]) + (g[:K, at + K : at + 2 * K] + g[K:, at + K : at + 2 * K])


def couple_kernel(
    n_sub, groups, layers, width,
    z_hbm, sig_hbm, sto_hbm, rows_hbm, cnt_hbm,
    bands_ref, lat_ref,
    z_ref, flat_ref, cut_ref, pick_ref, load_sem, sig_ref, sto_ref, rows_ref, cnt_ref, small_sem, sel_ref, lhs_ref, coef_ref, out_ref, in_ref, psig_out, psig_in, lay_out, lay_in, sig_out, sig_in,
    ret_out, ret_in, blk_ref, wgt_ref, hot_ref, own_band,
    send_sem, recv_sem, psig_send, psig_recv, lay_send, lay_recv, ret_send, ret_recv, band_send, band_recv,
):
    me = lax.axis_index("sub")
    level = lax.axis_index("coarse")
    cy = width // CX
    per = LANES // cy
    pad = rows_ref.shape[1]
    faces = cy * layers

    def load(c):
        return pltpu.make_async_copy(
            z_hbm.at[:, pl.ds(c * LANES, LANES)], z_ref.at[pl.ds(c * K * layers, K * layers)], load_sem.at[c]
        )

    small = [
        pltpu.make_async_copy(src, dst, small_sem.at[i])
        for i, (src, dst) in enumerate(
            ((sig_hbm, sig_ref), (rows_hbm, rows_ref), (sto_hbm, sto_ref), (cnt_hbm, cnt_ref))
        )
    ]
    for copy in small:
        copy.start()
    for c in range(width // LANES):
        load(c).start()

    def layer(z):
        return jnp.concatenate(
            [z_ref[pl.ds(c * K * layers + z, K, stride=layers), :] for c in range(width // LANES)], axis=1
        )

    def reachable(slot):
        other = me + offset_of(slot)
        return jnp.logical_and(other >= 0, other < n_sub)

    barrier = pltpu.get_barrier_semaphore()
    for slot in range(SLOTS):
        @pl.when(reachable(slot))
        def _():
            pl.semaphore_signal(barrier, inc=1, device_id={"sub": me + offset_of(slot)}, device_id_type=MESH)
    for step in range(1, groups):
        pl.semaphore_signal(
            barrier, inc=1, device_id={"coarse": lax.rem(level + step, groups)}, device_id_type=MESH
        )

    row = lax.broadcasted_iota(jnp.int32, (width, 2 * LANES), 0)
    lane = lax.broadcasted_iota(jnp.int32, (width, 2 * LANES), 1)
    cell = (lane % cy) * CX + jnp.where(lane >= LANES, CX - 1, 0)
    hit = row == cell
    part = (lane % LANES) // cy
    for i in range(per):
        sel_ref[i] = jnp.where(jnp.logical_and(hit, part == i), 1.0, 0.0).astype(jnp.bfloat16)

    for copy in small:
        copy.wait()
    sigma = sig_ref[...]
    sigma_split = split(sigma)
    placed = []
    for i in range(per):
        t = dot_nn(sigma_split, sel_ref[i])
        placed.append(t[:layers] + t[layers:])
    position = lax.broadcasted_iota(jnp.int32, (layers, width), 1)
    depth = lax.broadcasted_iota(jnp.int32, (layers, width), 0)
    wx = jnp.where(position % CX == CX - 1, 0.0, harmonic(sigma, pltpu.roll(sigma, width - 1, 1)))
    wy = jnp.where(position >= width - CX, 0.0, harmonic(sigma, pltpu.roll(sigma, width - CX, 1)))
    wz = jnp.where(depth == layers - 1, 0.0, harmonic(sigma, pltpu.roll(sigma, layers - 1, 0)))
    coef_ref[0] = 0.5 * (
        sto_ref[...] + (wx + pltpu.roll(wx, 1, 1)) + (wy + pltpu.roll(wy, CX, 1)) + (wz + pltpu.roll(wz, 1, 0))
    )
    coef_ref[1] = wx
    coef_ref[2] = wy
    coef_ref[3] = wz

    face_cell = lax.broadcasted_iota(jnp.int32, (faces, pad), 0)

    def onehot(slot):
        index = lax.shift_right_logical(rows_ref[slot : slot + 1, :], CX.bit_length() - 1)
        return jnp.where(face_cell == index, 1.0, 0.0).astype(jnp.bfloat16)

    for slot in range(1, SLOTS, 2):
        hot_ref[slot // 2] = onehot(slot)
    for c in range(width // LANES):
        load(c).wait()
    for g in range(layers // per):
        total = jnp.zeros((2 * K, 2 * LANES), jnp.float32)
        sig_row = jnp.zeros((1, 2 * LANES), jnp.float32)
        for i in range(per):
            z = g * per + i
            here = layer(z)
            flat_ref[z] = here
            cut = split(here)
            cut_ref[z] = cut
            total = total + dot_nn(cut, sel_ref[i])
            sig_row = sig_row + placed[i][z : z + 1]
        high, low = halves(sig_row)
        sig_rows = jnp.concatenate(
            [jnp.broadcast_to(high, (SUB, 2 * LANES)), jnp.broadcast_to(low, (SUB, 2 * LANES))], axis=0
        )
        stacked = jnp.concatenate([total, sig_rows], axis=0).astype(jnp.bfloat16)
        for f in range(2):
            lhs_ref[f, :, g * LANES : (g + 1) * LANES] = stacked[:, f * LANES : (f + 1) * LANES]

    lay_out[:K] = flat_ref[0]
    lay_out[K:] = jnp.broadcast_to(sigma[:1], (SUB, width))
    sig_out[...] = jnp.broadcast_to(sigma[layers - 1 :], (SUB, width))

    beside = jnp.minimum(me, REACH) + jnp.minimum(n_sub - 1 - me, REACH)
    pl.semaphore_wait(barrier, beside + groups - 1)

    def down():
        return pltpu.make_async_remote_copy(
            src_ref=lay_out, dst_ref=lay_in, send_sem=lay_send.at[0], recv_sem=lay_recv.at[0],
            device_id={"coarse": level - 1}, device_id_type=MESH,
        )

    def up():
        return pltpu.make_async_remote_copy(
            src_ref=sig_out, dst_ref=sig_in, send_sem=lay_send.at[1], recv_sem=lay_recv.at[1],
            device_id={"coarse": level + 1}, device_id_type=MESH,
        )

    @pl.when(level > 0)
    def _():
        down().start()

    @pl.when(level < groups - 1)
    def _():
        up().start()

    def picked_copy(slot):
        mirror = SLOTS - 1 - slot
        return pltpu.make_async_remote_copy(
            src_ref=out_ref.at[slot], dst_ref=in_ref.at[mirror // 2],
            send_sem=send_sem.at[slot // 2], recv_sem=recv_sem.at[mirror // 2],
            device_id={"sub": me + offset_of(slot)}, device_id_type=MESH,
        )

    def sigma_copy(slot):
        mirror = SLOTS - 1 - slot
        return pltpu.make_async_remote_copy(
            src_ref=psig_out.at[slot], dst_ref=psig_in.at[mirror],
            send_sem=psig_send.at[slot], recv_sem=psig_recv.at[mirror],
            device_id={"sub": me + offset_of(slot)}, device_id_type=MESH,
        )

    for batch in ((1, 7), (3, 5), (0, 2, 4, 6)):
        for slot in batch:
            hot = hot_ref[slot // 2] if slot % 2 else onehot(slot)
            picked = dot_nn(lhs_ref[0 if slot < REACH else 1], hot)
            out_ref[slot] = picked[:K] + picked[K : 2 * K]
            pick_ref[slot] = picked[: 2 * K].astype(jnp.bfloat16)
            psig_out[slot] = picked[2 * K : 2 * K + SUB] + picked[2 * K + SUB :]
        for slot in batch:
            @pl.when(reachable(slot))
            def _():
                if slot % 2:
                    picked_copy(slot).start()
                sigma_copy(slot).start()

    def some_layers(step, gram):
        start = step * per
        cells = [flat_ref[start + i] for i in range(per)]
        cells.append(flat_ref[jnp.minimum(start + per, layers - 1)])
        lefts, rights = [], []
        for i in range(per):
            z = start + i
            here = cells[i]
            applied = (
                coef_ref[0, pl.ds(z, 1), :] * here
                - coef_ref[1, pl.ds(z, 1), :] * pltpu.roll(here, width - 1, 1)
                - coef_ref[2, pl.ds(z, 1), :] * pltpu.roll(here, width - CX, 1)
                - coef_ref[3, pl.ds(z, 1), :] * cells[i + 1]
            )
            lefts.append(cut_ref[z])
            rights.append(split(applied))
        return gram + dot_nt(jnp.concatenate(lefts, axis=1), jnp.concatenate(rights, axis=1))

    gram = lax.fori_loop(0, layers // per, some_layers, jnp.zeros((2 * K, 2 * K), jnp.float32))
    half = quad(gram)
    own = half + half.T

    @pl.when(level < groups - 1)
    def _():
        down().wait_recv()

    @pl.when(level > 0)
    def _():
        up().wait_recv()

    for slot in range(SLOTS):
        @pl.when(reachable(slot))
        def _():
            sigma_copy(SLOTS - 1 - slot).wait_recv()

    has_above = level < groups - 1
    has_below = level > 0
    top = flat_ref[layers - 1]
    bottom = flat_ref[0]
    above = jnp.where(has_above, lay_in[:K], 0.0)
    upper = jnp.where(has_above, harmonic(sigma[layers - 1 :], lay_in[K : K + 1]), 0.0)
    lower = jnp.where(has_below, harmonic(sigma[:1], sig_in[:1]), 0.0)
    top_weighted = split(top * upper)
    upper_block = -quad(dot_nt(top_weighted, split(above)))
    spot = lax.broadcasted_iota(jnp.int32, (1, pad), 1)
    lefts = [top_weighted, split(bottom * lower)]
    rights = [cut_ref[layers - 1], cut_ref[0]]
    for slot in range(SLOTS):
        live = jnp.logical_and(spot < cnt_ref[0, 0, slot], reachable(slot))
        weight = jnp.where(live, harmonic(psig_out[slot, :1], psig_in[slot, :1]), 0.0)
        rows = out_ref[slot]
        lefts.append(split(rows * weight))
        rights.append(pick_ref[slot])
        if slot % 2 == 0:
            wgt_ref[slot // 2] = lefts[-1]
    own = own + quad(dot_nt(jnp.concatenate(lefts, axis=1), jnp.concatenate(rights, axis=1)))

    band = jnp.concatenate([own, upper_block], axis=1)
    own_band[...] = band

    def band_copy(step):
        return pltpu.make_async_remote_copy(
            src_ref=own_band, dst_ref=bands_ref.at[level],
            send_sem=band_send.at[step], recv_sem=band_recv.at[level],
            device_id={"coarse": lax.rem(level + step, groups)}, device_id_type=MESH,
        )

    for step in range(1, groups):
        band_copy(step).start()
    bands_ref[level] = band

    def ret_copy(slot):
        return pltpu.make_async_remote_copy(
            src_ref=ret_out.at[slot], dst_ref=ret_in.at[SLOTS - 1 - slot],
            send_sem=ret_send.at[slot], recv_sem=ret_recv.at[SLOTS - 1 - slot],
            device_id={"sub": me + offset_of(slot)}, device_id_type=MESH,
        )

    def ret_arrival(slot):
        return pltpu.make_async_remote_copy(
            src_ref=ret_out.at[SLOTS - 1 - slot], dst_ref=ret_in.at[slot],
            send_sem=ret_send.at[SLOTS - 1 - slot], recv_sem=ret_recv.at[slot],
            device_id={"sub": me + offset_of(slot)}, device_id_type=MESH,
        )

    for slot in range(0, SLOTS, 2):
        @pl.when(reachable(slot))
        def _():
            picked_copy(SLOTS - 1 - slot).wait_recv()

    wide = jnp.zeros((K, LANES - K), jnp.float32)
    for slot in range(0, SLOTS, 2):
        partner = jnp.where(reachable(slot), in_ref[slot // 2], 0.0)
        block = -quad(dot_nt(wgt_ref[slot // 2], split(partner)))
        blk_ref[slot] = block
        ret_out[slot] = jnp.concatenate([block.T, wide], axis=1)
    for slot in range(0, SLOTS, 2):
        @pl.when(reachable(slot))
        def _():
            ret_copy(slot).start()

    for slot in range(SLOTS):
        if slot % 2:
            @pl.when(reachable(slot))
            def _():
                ret_arrival(slot).wait_recv()

            blk_ref[slot] = jnp.where(reachable(slot), ret_in[slot, :, :K], 0.0)
    for pair in range(SLOTS // 2):
        lat_ref[:, pair * 2 * K : (pair + 1) * 2 * K] = jnp.concatenate(
            [blk_ref[2 * pair], blk_ref[2 * pair + 1]], axis=1
        )
    for step in range(1, groups):
        source = lax.rem(level + groups - step, groups)
        pltpu.make_async_remote_copy(
            src_ref=own_band, dst_ref=bands_ref.at[source],
            send_sem=band_send.at[step], recv_sem=band_recv.at[source],
            device_id={"coarse": source}, device_id_type=MESH,
        ).wait_recv()
    for step in range(1, groups):
        band_copy(step).wait_send()
    for slot in range(SLOTS):
        @pl.when(reachable(slot))
        def _():
            sigma_copy(slot).wait_send()
            if slot % 2:
                picked_copy(slot).wait_send()
            else:
                ret_copy(slot).wait_send()

    @pl.when(level > 0)
    def _():
        down().wait_send()

    @pl.when(level < groups - 1)
    def _():
        up().wait_send()


def spread(x, at):
    return jnp.broadcast_to(x[at : at + 1, :], x.shape)


def column(x, at):
    return jnp.broadcast_to(x[:, at : at + 1], (x.shape[0], LANES))


def eliminate(left, right):
    left, right = list(left), list(right)
    below = lax.broadcasted_iota(jnp.int32, (SUB, LANES), 0)
    for p in range(K // SUB):
        cols = [[column(left[g], p * SUB + j) for j in range(SUB)] for g in range(p, K // SUB)]
        head = cols[0]
        a, b = left[p], right[p]
        inverses, above, rows_a, rows_b, roots = [], [], [], [], []
        for j in range(0, SUB, 2):
            first, cross, second = spread(head[j], j), spread(head[j + 1], j), spread(head[j + 1], j + 1)
            inverse_1 = 1.0 / first
            inverse_2 = first * (1.0 / (first * second - cross * cross))
            ratio = cross * inverse_1
            scale_1 = jnp.where(below > j, head[j], 0.0) * inverse_1
            scale_2 = jnp.where(below > j + 1, head[j + 1] - scale_1 * cross, 0.0) * inverse_2

            def pair(x):
                top = spread(x, j)
                return top, spread(x, j + 1) - ratio * top

            entries_1, entries_2 = {j + 1: cross}, {}
            for k in range(j + 2, SUB):
                entries_1[k], entries_2[k] = pair(head[k])
                head[k] = (head[k] - scale_1 * entries_1[k]) - scale_2 * entries_2[k]
            inverses += [inverse_1, inverse_2]
            roots += [lax.rsqrt(first), lax.rsqrt(second - ratio * cross)]
            above += [entries_1, entries_2]
            top_a, next_a = pair(a)
            top_b, next_b = pair(b)
            a = (a - scale_1 * top_a) - scale_2 * next_a
            b = (b - scale_1 * top_b) - scale_2 * next_b
            rows_a += [top_a, next_a]
            rows_b += [top_b, next_b]
        left[p], right[p] = a, b
        for g in range(p + 1, K // SUB):
            tail = cols[g - p]
            la, lb = left[g], right[g]
            for j in range(SUB):
                scale = tail[j] * inverses[j]
                for k in range(j + 1, SUB):
                    tail[k] = tail[k] - scale * above[j][k]
                la = la - scale * rows_a[j]
                lb = lb - scale * rows_b[j]
            left[g], right[g] = la, lb
        for j in range(SUB):
            left[p] = jnp.where(below == j, left[p] * roots[j], left[p])
            right[p] = jnp.where(below == j, right[p] * roots[j], right[p])
    return left, right


def thirds(x):
    high, rest = halves(x)
    middle, low = halves(rest)
    return high, middle, low


def exact_tn(left, right):
    a, b, c = thirds(left)
    d, e, f = thirds(right)
    return lax.dot_general(
        jnp.concatenate([a, a, b, b, a, c], axis=0).astype(jnp.bfloat16),
        jnp.concatenate([d, e, d, e, f, d], axis=0).astype(jnp.bfloat16),
        (((0,), (0,)), ((), ())), preferred_element_type=jnp.float32,
    )


def factor_kernel(
    groups, bands_ref, lat_ref, factor_ref, panel_ref, low_ref, inv_ref, turn_ref, schur_ref, last_ref, scaled_ref, fit_ref
):
    level = lax.axis_index("coarse")
    row = lax.broadcasted_iota(jnp.int32, (K, LANES), 0)
    lane = lax.broadcasted_iota(jnp.int32, (K, LANES), 1)
    eye = jnp.where(row == lane, 1.0, 0.0)
    fit = []
    for k in range(groups):
        diagonal = jnp.where(row == lane, bands_ref[k], 0.0)
        fit.append((jnp.sum(diagonal, axis=0, keepdims=True)[:, :K], jnp.sum(diagonal, axis=1, keepdims=True)))
    for k in range(groups):
        after = fit[k + 1][0] if k + 1 < groups else jnp.ones((1, K), jnp.float32)
        along = jnp.concatenate([fit[k][0], after], axis=1)
        shrink = lax.rsqrt(along)
        scaled_ref[k] = bands_ref[k] * shrink * lax.rsqrt(fit[k][1])
        fit_ref[k, :1] = along * shrink
        fit_ref[k, 1:2] = shrink
    schur_ref[...] = jnp.zeros_like(schur_ref)
    last_ref[...] = jnp.zeros_like(last_ref)
    low_ref[0] = jnp.zeros_like(low_ref[0])
    inv_ref[0] = jnp.zeros_like(inv_ref[0])
    turn_ref[0] = jnp.zeros_like(turn_ref[0])

    def panel_block(k, before):
        right = jnp.where(level == k, lat_ref[...], 0.0) - exact_tn(turn_ref[before], last_ref[...])
        return exact_tn(inv_ref[jnp.maximum(k, 0)], right)

    def one_block(k, carry):
        done = jnp.maximum(k - 1, 0)
        last = panel_block(k - 1, jnp.maximum(k - 2, 0))
        start = scaled_ref[k] - schur_ref[...]
        tiles = [start[g * SUB : (g + 1) * SUB] for g in range(K // SUB)]
        ones = [eye[g * SUB : (g + 1) * SUB] for g in range(K // SUB)]
        left, right = eliminate(tiles, ones)
        left = jnp.concatenate(left, axis=0)
        right = jnp.concatenate(right, axis=0)
        left = jnp.where(lane >= row, left, 0.0)
        turn = left[:, K:]
        real_turn = (left * fit_ref[k, :1])[:, K:]
        last_ref[...] = last
        panel_ref[0, 0, pl.ds(pl.multiple_of(done * K, K), K), :] = last
        low_ref[k] = (left * fit_ref[k, :1]).T
        inv_ref[k] = (right * fit_ref[k, 1:2]).T[:K]
        turn_ref[k] = real_turn
        schur_ref[:, :K] = exact_tn(turn, turn)
        return carry

    factor_ref[0] = jnp.zeros_like(factor_ref[0])
    lax.fori_loop(0, groups, one_block, 0)
    panel_ref[0, 0, (groups - 1) * K :, :] = panel_block(groups - 1, groups - 2)
    for k in range(groups):
        factor_ref[0, k * K : (k + 1) * K, k * K : (k + 1) * K] = low_ref[k, :K]
        if k + 1 < groups:
            factor_ref[0, (k + 1) * K : (k + 2) * K, k * K : (k + 1) * K] = low_ref[k, K:]


def body(n_sub, groups, deflation, conductivity, storage, interface_rows, interface_counts):
    layers, width = deflation.shape[2], deflation.shape[3]
    pad = interface_rows.shape[3]
    faces = width // CX * layers
    f32 = jnp.float32
    vmem = pl.BlockSpec(memory_space=pltpu.VMEM)
    dma = pltpu.SemaphoreType.DMA
    bands, lateral = pl.pallas_call(
        functools.partial(couple_kernel, n_sub, groups, layers, width),
        out_shape=(
            jax.ShapeDtypeStruct((groups, K, 2 * K), f32),
            jax.ShapeDtypeStruct((K, SLOTS * K), f32),
        ),
        in_specs=[pl.BlockSpec(memory_space=pltpu.HBM)] * 5,
        out_specs=(vmem, vmem),
        scratch_shapes=[
            pltpu.VMEM((width // LANES * K * layers, LANES), f32),
            pltpu.VMEM((layers, K, width), f32),
            pltpu.VMEM((layers, 2 * K, width), jnp.bfloat16),
            pltpu.VMEM((SLOTS, 2 * K, pad), jnp.bfloat16),
            dma((width // LANES,)),
            pltpu.VMEM((layers, width), f32),
            pltpu.VMEM((layers, width), f32),
            pltpu.VMEM((SLOTS, pad), jnp.int32),
            pltpu.SMEM((1, 1, SLOTS), jnp.int32),
            dma((4,)),
            pltpu.VMEM((LANES * CX // width, width, 2 * LANES), jnp.bfloat16),
            pltpu.VMEM((2, 2 * K + 2 * SUB, faces), jnp.bfloat16),
            pltpu.VMEM((4, layers, width), f32),
            pltpu.VMEM((SLOTS, K, pad), f32),
            pltpu.VMEM((REACH, K, pad), f32),
            pltpu.VMEM((SLOTS, SUB, pad), f32),
            pltpu.VMEM((SLOTS, SUB, pad), f32),
            pltpu.VMEM((K + SUB, width), f32),
            pltpu.VMEM((K + SUB, width), f32),
            pltpu.VMEM((SUB, width), f32),
            pltpu.VMEM((SUB, width), f32),
            pltpu.VMEM((SLOTS, K, LANES), f32),
            pltpu.VMEM((SLOTS, K, LANES), f32),
            pltpu.VMEM((SLOTS, K, K), f32),
            pltpu.VMEM((REACH, 2 * K, pad), jnp.bfloat16),
            pltpu.VMEM((REACH, faces, pad), jnp.bfloat16),
            pltpu.VMEM((K, 2 * K), f32),
            dma((REACH,)), dma((REACH,)), dma((SLOTS,)), dma((SLOTS,)), dma((2,)), dma((2,)),
            dma((SLOTS,)), dma((SLOTS,)), dma((groups,)), dma((groups,)),
        ],
        compiler_params=pltpu.CompilerParams(
            collective_id=0, has_side_effects=True, vmem_limit_bytes=40 * 1024 * 1024
        ),
        name="couple",
    )(
        *(
            pltpu.with_memory_space_constraint(x, pltpu.HBM)
            for x in (
                deflation.reshape(K * layers, width), conductivity[0], storage[0],
                interface_rows[0, 0], interface_counts,
            )
        )
    )
    return pl.pallas_call(
        functools.partial(factor_kernel, groups),
        out_shape=(
            jax.ShapeDtypeStruct((1, groups * K, groups * K), f32),
            jax.ShapeDtypeStruct((1, 1, groups * K, SLOTS * K), f32),
        ),
        in_specs=[vmem, vmem],
        out_specs=(vmem, vmem),
        scratch_shapes=[
            pltpu.VMEM((groups, 2 * K, K), f32),
            pltpu.VMEM((groups, K, K), f32),
            pltpu.VMEM((groups, K, K), f32),
            pltpu.VMEM((K, LANES), f32),
            pltpu.VMEM((K, SLOTS * K), f32),
            pltpu.VMEM((groups, K, LANES), f32),
            pltpu.VMEM((groups, SUB, LANES), f32),
        ],
        compiler_params=pltpu.CompilerParams(vmem_limit_bytes=40 * 1024 * 1024),
        name="factor",
    )(bands, lateral)


def solution(mesh):
    placed = (
        P("sub", None, "coarse", None),
        P("sub", "coarse", None),
        P("sub", "coarse", None),
        P("sub", "coarse", None, None),
        P("sub", "coarse", None),
    )
    return jax.shard_map(
        functools.partial(body, mesh.shape["sub"], mesh.shape["coarse"]),
        mesh=mesh,
        in_specs=placed,
        out_specs=(P("sub", None, None), P("sub", "coarse", None, None)),
        check_vma=False,
    )
```

```python
import functools

import jax
import jax.numpy as jnp
from jax import lax
from jax.experimental import pallas as pl
from jax.experimental.pallas import tpu as pltpu
from jax.sharding import PartitionSpec as P

K = 64
CX = 16
REACH = 4
LANES = 128
SUB = 8
SLOTS = 2 * REACH
MESH = pl.DeviceIdType.MESH


def harmonic(first, second):
    return 2.0 * first * second / (first + second)


def offset_of(slot):
    return slot - REACH if slot < REACH else slot - REACH + 1


def halves(x):
    high = x.astype(jnp.bfloat16).astype(jnp.float32)
    return high, x - high


def split(x):
    return jnp.concatenate(halves(x), axis=0).astype(jnp.bfloat16)


def dot_nn(left, right):
    return lax.dot_general(left, right, (((1,), (0,)), ((), ())), preferred_element_type=jnp.float32)


def dot_nt(left, right):
    return lax.dot_general(left, right, (((1,), (1,)), ((), ())), preferred_element_type=jnp.float32)


def quad(g, at=0):
    return (g[:K, at : at + K] + g[K:, at : at + K]) + (g[:K, at + K : at + 2 * K] + g[K:, at + K : at + 2 * K])


def spread(x, at):
    return jnp.broadcast_to(x[at : at + 1, :], x.shape)


def column(x, at):
    return jnp.broadcast_to(x[:, at : at + 1], (x.shape[0], LANES))


def eliminate(left, right):
    left, right = list(left), list(right)
    below = lax.broadcasted_iota(jnp.int32, (SUB, LANES), 0)
    for p in range(K // SUB):
        cols = [[column(left[g], p * SUB + j) for j in range(SUB)] for g in range(p, K // SUB)]
        head = cols[0]
        a, b = left[p], right[p]
        inverses, above, rows_a, rows_b, roots = [], [], [], [], []
        for j in range(0, SUB, 2):
            first, cross, second = spread(head[j], j), spread(head[j + 1], j), spread(head[j + 1], j + 1)
            inverse_1 = 1.0 / first
            inverse_2 = first * (1.0 / (first * second - cross * cross))
            ratio = cross * inverse_1
            scale_1 = jnp.where(below > j, head[j], 0.0) * inverse_1
            scale_2 = jnp.where(below > j + 1, head[j + 1] - scale_1 * cross, 0.0) * inverse_2

            def pair(x):
                top = spread(x, j)
                return top, spread(x, j + 1) - ratio * top

            entries_1, entries_2 = {j + 1: cross}, {}
            for k in range(j + 2, SUB):
                entries_1[k], entries_2[k] = pair(head[k])
                head[k] = (head[k] - scale_1 * entries_1[k]) - scale_2 * entries_2[k]
            inverses += [inverse_1, inverse_2]
            roots += [lax.rsqrt(first), lax.rsqrt(second - ratio * cross)]
            above += [entries_1, entries_2]
            top_a, next_a = pair(a)
            top_b, next_b = pair(b)
            a = (a - scale_1 * top_a) - scale_2 * next_a
            b = (b - scale_1 * top_b) - scale_2 * next_b
            rows_a += [top_a, next_a]
            rows_b += [top_b, next_b]
        left[p], right[p] = a, b
        for g in range(p + 1, K // SUB):
            tail = cols[g - p]
            la, lb = left[g], right[g]
            for j in range(SUB):
                scale = tail[j] * inverses[j]
                for k in range(j + 1, SUB):
                    tail[k] = tail[k] - scale * above[j][k]
                la = la - scale * rows_a[j]
                lb = lb - scale * rows_b[j]
            left[g], right[g] = la, lb
        for j in range(SUB):
            left[p] = jnp.where(below == j, left[p] * roots[j], left[p])
            right[p] = jnp.where(below == j, right[p] * roots[j], right[p])
    return left, right


def thirds(x):
    high, rest = halves(x)
    middle, low = halves(rest)
    return high, middle, low


def exact_tn(left, right):
    a, b, c = thirds(left)
    d, e, f = thirds(right)
    return lax.dot_general(
        jnp.concatenate([a, a, b, b, a, c], axis=0).astype(jnp.bfloat16),
        jnp.concatenate([d, e, d, e, f, d], axis=0).astype(jnp.bfloat16),
        (((0,), (0,)), ((), ())), preferred_element_type=jnp.float32,
    )


def couple_kernel(
    n_sub, groups, layers, width,
    z_hbm, sig_hbm, sto_hbm, rows_hbm, cnt_hbm,
    factor_ref, panel_ref,
    bands_ref, lat_ref, low_ref, inv_ref, turn_ref, schur_ref, last_ref, scaled_ref, fit_ref,
    z_ref, load_sem, sig_ref, sto_ref, rows_ref, cnt_ref, small_sem, sel_ref, lhs_ref, coef_ref, out_ref, in_ref, psig_out, psig_in, lay_out, lay_in, sig_out, sig_in,
    ret_out, ret_in, blk_ref, wgt_ref, hot_ref, own_band,
    send_sem, recv_sem, psig_send, psig_recv, lay_send, lay_recv, ret_send, ret_recv, band_send, band_recv,
):
    me = lax.axis_index("sub")
    level = lax.axis_index("coarse")
    cy = width // CX
    per = LANES // cy
    pad = rows_ref.shape[1]
    faces = cy * layers

    def load(c):
        return pltpu.make_async_copy(
            z_hbm.at[:, pl.ds(c * LANES, LANES)], z_ref.at[pl.ds(c * K * layers, K * layers)], load_sem.at[c]
        )

    small = [
        pltpu.make_async_copy(src, dst, small_sem.at[i])
        for i, (src, dst) in enumerate(
            ((sig_hbm, sig_ref), (rows_hbm, rows_ref), (sto_hbm, sto_ref), (cnt_hbm, cnt_ref))
        )
    ]
    for copy in small:
        copy.start()
    for c in range(width // LANES):
        load(c).start()

    def layer(z):
        return jnp.concatenate(
            [z_ref[pl.ds(c * K * layers + z, K, stride=layers), :] for c in range(width // LANES)], axis=1
        )

    def reachable(slot):
        other = me + offset_of(slot)
        return jnp.logical_and(other >= 0, other < n_sub)

    barrier = pltpu.get_barrier_semaphore()
    for slot in range(SLOTS):
        @pl.when(reachable(slot))
        def _():
            pl.semaphore_signal(barrier, inc=1, device_id={"sub": me + offset_of(slot)}, device_id_type=MESH)
    for step in range(1, groups):
        pl.semaphore_signal(
            barrier, inc=1, device_id={"coarse": lax.rem(level + step, groups)}, device_id_type=MESH
        )

    row = lax.broadcasted_iota(jnp.int32, (width, 2 * LANES), 0)
    lane = lax.broadcasted_iota(jnp.int32, (width, 2 * LANES), 1)
    cell = (lane % cy) * CX + jnp.where(lane >= LANES, CX - 1, 0)
    hit = row == cell
    part = (lane % LANES) // cy
    for i in range(per):
        sel_ref[i] = jnp.where(jnp.logical_and(hit, part == i), 1.0, 0.0).astype(jnp.bfloat16)

    for copy in small:
        copy.wait()
    sigma = sig_ref[...]
    sigma_split = split(sigma)
    placed = []
    for i in range(per):
        t = dot_nn(sigma_split, sel_ref[i])
        placed.append(t[:layers] + t[layers:])
    position = lax.broadcasted_iota(jnp.int32, (layers, width), 1)
    depth = lax.broadcasted_iota(jnp.int32, (layers, width), 0)
    wx = jnp.where(position % CX == CX - 1, 0.0, harmonic(sigma, pltpu.roll(sigma, width - 1, 1)))
    wy = jnp.where(position >= width - CX, 0.0, harmonic(sigma, pltpu.roll(sigma, width - CX, 1)))
    wz = jnp.where(depth == layers - 1, 0.0, harmonic(sigma, pltpu.roll(sigma, layers - 1, 0)))
    coef_ref[0] = 0.5 * (
        sto_ref[...] + (wx + pltpu.roll(wx, 1, 1)) + (wy + pltpu.roll(wy, CX, 1)) + (wz + pltpu.roll(wz, 1, 0))
    )
    coef_ref[1] = wx
    coef_ref[2] = wy
    coef_ref[3] = wz

    face_cell = lax.broadcasted_iota(jnp.int32, (faces, pad), 0)

    def onehot(slot):
        index = lax.shift_right_logical(rows_ref[slot : slot + 1, :], CX.bit_length() - 1)
        return jnp.where(face_cell == index, 1.0, 0.0).astype(jnp.bfloat16)

    for slot in range(1, SLOTS, 2):
        hot_ref[slot // 2] = onehot(slot)
    for c in range(width // LANES):
        load(c).wait()
    for g in range(layers // per):
        total = jnp.zeros((2 * K, 2 * LANES), jnp.float32)
        sig_row = jnp.zeros((1, 2 * LANES), jnp.float32)
        for i in range(per):
            z = g * per + i
            total = total + dot_nn(split(layer(z)), sel_ref[i])
            sig_row = sig_row + placed[i][z : z + 1]
        high, low = halves(sig_row)
        sig_rows = jnp.concatenate(
            [jnp.broadcast_to(high, (SUB, 2 * LANES)), jnp.broadcast_to(low, (SUB, 2 * LANES))], axis=0
        )
        stacked = jnp.concatenate([total, sig_rows], axis=0).astype(jnp.bfloat16)
        for f in range(2):
            lhs_ref[f, :, g * LANES : (g + 1) * LANES] = stacked[:, f * LANES : (f + 1) * LANES]

    lay_out[:K] = layer(0)
    lay_out[K:] = jnp.broadcast_to(sigma[:1], (SUB, width))
    sig_out[...] = jnp.broadcast_to(sigma[layers - 1 :], (SUB, width))

    beside = jnp.minimum(me, REACH) + jnp.minimum(n_sub - 1 - me, REACH)
    pl.semaphore_wait(barrier, beside + groups - 1)

    def down():
        return pltpu.make_async_remote_copy(
            src_ref=lay_out, dst_ref=lay_in, send_sem=lay_send.at[0], recv_sem=lay_recv.at[0],
            device_id={"coarse": level - 1}, device_id_type=MESH,
        )

    def up():
        return pltpu.make_async_remote_copy(
            src_ref=sig_out, dst_ref=sig_in, send_sem=lay_send.at[1], recv_sem=lay_recv.at[1],
            device_id={"coarse": level + 1}, device_id_type=MESH,
        )

    @pl.when(level > 0)
    def _():
        down().start()

    @pl.when(level < groups - 1)
    def _():
        up().start()

    def picked_copy(slot):
        mirror = SLOTS - 1 - slot
        return pltpu.make_async_remote_copy(
            src_ref=out_ref.at[slot], dst_ref=in_ref.at[mirror // 2],
            send_sem=send_sem.at[slot // 2], recv_sem=recv_sem.at[mirror // 2],
            device_id={"sub": me + offset_of(slot)}, device_id_type=MESH,
        )

    def sigma_copy(slot):
        mirror = SLOTS - 1 - slot
        return pltpu.make_async_remote_copy(
            src_ref=psig_out.at[slot], dst_ref=psig_in.at[mirror],
            send_sem=psig_send.at[slot], recv_sem=psig_recv.at[mirror],
            device_id={"sub": me + offset_of(slot)}, device_id_type=MESH,
        )

    for batch in ((1, 7), (3, 5), (0, 2, 4, 6)):
        for slot in batch:
            hot = hot_ref[slot // 2] if slot % 2 else onehot(slot)
            picked = dot_nn(lhs_ref[0 if slot < REACH else 1], hot)
            out_ref[slot] = picked[:K] + picked[K : 2 * K]
            psig_out[slot] = picked[2 * K : 2 * K + SUB] + picked[2 * K + SUB :]
        for slot in batch:
            @pl.when(reachable(slot))
            def _():
                if slot % 2:
                    picked_copy(slot).start()
                sigma_copy(slot).start()

    def some_layers(step, gram):
        start = step * per
        cells = [layer(start + i) for i in range(per)]
        cells.append(layer(jnp.minimum(start + per, layers - 1)))
        lefts, rights = [], []
        for i in range(per):
            z = start + i
            here = cells[i]
            applied = (
                coef_ref[0, pl.ds(z, 1), :] * here
                - coef_ref[1, pl.ds(z, 1), :] * pltpu.roll(here, width - 1, 1)
                - coef_ref[2, pl.ds(z, 1), :] * pltpu.roll(here, width - CX, 1)
                - coef_ref[3, pl.ds(z, 1), :] * cells[i + 1]
            )
            lefts.append(split(here))
            rights.append(split(applied))
        return gram + dot_nt(jnp.concatenate(lefts, axis=1), jnp.concatenate(rights, axis=1))

    gram = lax.fori_loop(0, layers // per, some_layers, jnp.zeros((2 * K, 2 * K), jnp.float32))
    half = quad(gram)
    own = half + half.T

    @pl.when(level < groups - 1)
    def _():
        down().wait_recv()

    @pl.when(level > 0)
    def _():
        up().wait_recv()

    for slot in range(SLOTS):
        @pl.when(reachable(slot))
        def _():
            sigma_copy(SLOTS - 1 - slot).wait_recv()

    has_above = level < groups - 1
    has_below = level > 0
    top = layer(layers - 1)
    bottom = layer(0)
    above = jnp.where(has_above, lay_in[:K], 0.0)
    upper = jnp.where(has_above, harmonic(sigma[layers - 1 :], lay_in[K : K + 1]), 0.0)
    lower = jnp.where(has_below, harmonic(sigma[:1], sig_in[:1]), 0.0)
    top_weighted = split(top * upper)
    upper_block = -quad(dot_nt(top_weighted, split(above)))
    spot = lax.broadcasted_iota(jnp.int32, (1, pad), 1)
    lefts = [top_weighted, split(bottom * lower)]
    rights = [split(top), split(bottom)]
    for slot in range(SLOTS):
        live = jnp.logical_and(spot < cnt_ref[0, 0, slot], reachable(slot))
        weight = jnp.where(live, harmonic(psig_out[slot, :1], psig_in[slot, :1]), 0.0)
        rows = out_ref[slot]
        lefts.append(split(rows * weight))
        rights.append(split(rows))
        if slot % 2 == 0:
            wgt_ref[slot // 2] = lefts[-1]
    own = own + quad(dot_nt(jnp.concatenate(lefts, axis=1), jnp.concatenate(rights, axis=1)))

    band = jnp.concatenate([own, upper_block], axis=1)
    own_band[...] = band

    def band_copy(step):
        return pltpu.make_async_remote_copy(
            src_ref=own_band, dst_ref=bands_ref.at[level],
            send_sem=band_send.at[step], recv_sem=band_recv.at[level],
            device_id={"coarse": lax.rem(level + step, groups)}, device_id_type=MESH,
        )

    for step in range(1, groups):
        band_copy(step).start()
    bands_ref[level] = band

    def ret_copy(slot):
        return pltpu.make_async_remote_copy(
            src_ref=ret_out.at[slot], dst_ref=ret_in.at[SLOTS - 1 - slot],
            send_sem=ret_send.at[slot], recv_sem=ret_recv.at[SLOTS - 1 - slot],
            device_id={"sub": me + offset_of(slot)}, device_id_type=MESH,
        )

    def ret_arrival(slot):
        return pltpu.make_async_remote_copy(
            src_ref=ret_out.at[SLOTS - 1 - slot], dst_ref=ret_in.at[slot],
            send_sem=ret_send.at[SLOTS - 1 - slot], recv_sem=ret_recv.at[slot],
            device_id={"sub": me + offset_of(slot)}, device_id_type=MESH,
        )

    for step in range(1, groups):
        source = lax.rem(level + groups - step, groups)
        pltpu.make_async_remote_copy(
            src_ref=own_band, dst_ref=bands_ref.at[source],
            send_sem=band_send.at[step], recv_sem=band_recv.at[source],
            device_id={"coarse": source}, device_id_type=MESH,
        ).wait_recv()
    row_id = lax.broadcasted_iota(jnp.int32, (K, LANES), 0)
    lane_id = lax.broadcasted_iota(jnp.int32, (K, LANES), 1)
    eye = jnp.where(row_id == lane_id, 1.0, 0.0)
    fit = []
    for k in range(groups):
        diagonal = jnp.where(row_id == lane_id, bands_ref[k], 0.0)
        fit.append((jnp.sum(diagonal, axis=0, keepdims=True)[:, :K], jnp.sum(diagonal, axis=1, keepdims=True)))
    for k in range(groups):
        after = fit[k + 1][0] if k + 1 < groups else jnp.ones((1, K), jnp.float32)
        along = jnp.concatenate([fit[k][0], after], axis=1)
        shrink = lax.rsqrt(along)
        scaled_ref[k] = bands_ref[k] * shrink * lax.rsqrt(fit[k][1])
        fit_ref[k, :1] = along * shrink
        fit_ref[k, 1:2] = shrink
    schur_ref[...] = jnp.zeros_like(schur_ref)
    last_ref[...] = jnp.zeros_like(last_ref)

    def panel_block(k, before):
        right = jnp.where(level == k, lat_ref[...], 0.0) - exact_tn(turn_ref[before], last_ref[...])
        return exact_tn(inv_ref[k], right)

    def one_block(k, carry):
        last = panel_block(k - 2, jnp.maximum(k - 3, 0)) if carry is not None else None
        start = scaled_ref[k] - schur_ref[...]
        tiles = [start[g * SUB : (g + 1) * SUB] for g in range(K // SUB)]
        ones = [eye[g * SUB : (g + 1) * SUB] for g in range(K // SUB)]
        left, right = eliminate(tiles, ones)
        left = jnp.concatenate(left, axis=0)
        right = jnp.concatenate(right, axis=0)
        left = jnp.where(lane_id >= row_id, left, 0.0)
        turn = left[:, K:]
        real_turn = (left * fit_ref[k, :1])[:, K:]
        if last is not None:
            last_ref[...] = last
            panel_ref[0, 0, pl.ds(pl.multiple_of((k - 2) * K, K), K), :] = last
        low_ref[k] = (left * fit_ref[k, :1]).T
        inv_ref[k] = (right * fit_ref[k, 1:2]).T[:K]
        turn_ref[k] = real_turn
        schur_ref[:, :K] = exact_tn(turn, turn)
        return carry

    factor_ref[0] = jnp.zeros_like(factor_ref[0])
    one_block(0, None)
    for slot in range(0, SLOTS, 2):
        @pl.when(reachable(slot))
        def _():
            picked_copy(SLOTS - 1 - slot).wait_recv()

    wide = jnp.zeros((K, LANES - K), jnp.float32)
    for slot in range(0, SLOTS, 2):
        partner = jnp.where(reachable(slot), in_ref[slot // 2], 0.0)
        block = -quad(dot_nt(wgt_ref[slot // 2], split(partner)))
        blk_ref[slot] = block
        ret_out[slot] = jnp.concatenate([block.T, wide], axis=1)
    for slot in range(0, SLOTS, 2):
        @pl.when(reachable(slot))
        def _():
            ret_copy(slot).start()

    one_block(1, None)
    for slot in range(SLOTS):
        if slot % 2:
            @pl.when(reachable(slot))
            def _():
                ret_arrival(slot).wait_recv()

            blk_ref[slot] = jnp.where(reachable(slot), ret_in[slot, :, :K], 0.0)
    for pair in range(SLOTS // 2):
        lat_ref[:, pair * 2 * K : (pair + 1) * 2 * K] = jnp.concatenate(
            [blk_ref[2 * pair], blk_ref[2 * pair + 1]], axis=1
        )
    lax.fori_loop(2, groups, one_block, 0)
    for k in range(groups - 2, groups):
        last = panel_block(k, max(k - 1, 0))
        last_ref[...] = last
        panel_ref[0, 0, k * K : (k + 1) * K, :] = last
    for k in range(groups):
        factor_ref[0, k * K : (k + 1) * K, k * K : (k + 1) * K] = low_ref[k, :K]
        if k + 1 < groups:
            factor_ref[0, (k + 1) * K : (k + 2) * K, k * K : (k + 1) * K] = low_ref[k, K:]
    for step in range(1, groups):
        band_copy(step).wait_send()
    for slot in range(SLOTS):
        @pl.when(reachable(slot))
        def _():
            sigma_copy(slot).wait_send()
            if slot % 2:
                picked_copy(slot).wait_send()
            else:
                ret_copy(slot).wait_send()

    @pl.when(level > 0)
    def _():
        down().wait_send()

    @pl.when(level < groups - 1)
    def _():
        up().wait_send()


def body(n_sub, groups, deflation, conductivity, storage, interface_rows, interface_counts):
    layers, width = deflation.shape[2], deflation.shape[3]
    pad = interface_rows.shape[3]
    faces = width // CX * layers
    f32 = jnp.float32
    vmem = pl.BlockSpec(memory_space=pltpu.VMEM)
    dma = pltpu.SemaphoreType.DMA
    return pl.pallas_call(
        functools.partial(couple_kernel, n_sub, groups, layers, width),
        out_shape=(
            jax.ShapeDtypeStruct((1, groups * K, groups * K), f32),
            jax.ShapeDtypeStruct((1, 1, groups * K, SLOTS * K), f32),
        ),
        in_specs=[pl.BlockSpec(memory_space=pltpu.HBM)] * 5,
        out_specs=(vmem, vmem),
        scratch_shapes=[
            pltpu.VMEM((groups, K, 2 * K), f32),
            pltpu.VMEM((K, SLOTS * K), f32),
            pltpu.VMEM((groups, 2 * K, K), f32),
            pltpu.VMEM((groups, K, K), f32),
            pltpu.VMEM((groups, K, K), f32),
            pltpu.VMEM((K, LANES), f32),
            pltpu.VMEM((K, SLOTS * K), f32),
            pltpu.VMEM((groups, K, LANES), f32),
            pltpu.VMEM((groups, SUB, LANES), f32),
            pltpu.VMEM((width // LANES * K * layers, LANES), f32),
            dma((width // LANES,)),
            pltpu.VMEM((layers, width), f32),
            pltpu.VMEM((layers, width), f32),
            pltpu.VMEM((SLOTS, pad), jnp.int32),
            pltpu.SMEM((1, 1, SLOTS), jnp.int32),
            dma((4,)),
            pltpu.VMEM((LANES * CX // width, width, 2 * LANES), jnp.bfloat16),
            pltpu.VMEM((2, 2 * K + 2 * SUB, faces), jnp.bfloat16),
            pltpu.VMEM((4, layers, width), f32),
            pltpu.VMEM((SLOTS, K, pad), f32),
            pltpu.VMEM((REACH, K, pad), f32),
            pltpu.VMEM((SLOTS, SUB, pad), f32),
            pltpu.VMEM((SLOTS, SUB, pad), f32),
            pltpu.VMEM((K + SUB, width), f32),
            pltpu.VMEM((K + SUB, width), f32),
            pltpu.VMEM((SUB, width), f32),
            pltpu.VMEM((SUB, width), f32),
            pltpu.VMEM((SLOTS, K, LANES), f32),
            pltpu.VMEM((SLOTS, K, LANES), f32),
            pltpu.VMEM((SLOTS, K, K), f32),
            pltpu.VMEM((REACH, 2 * K, pad), jnp.bfloat16),
            pltpu.VMEM((REACH, faces, pad), jnp.bfloat16),
            pltpu.VMEM((K, 2 * K), f32),
            dma((REACH,)), dma((REACH,)), dma((SLOTS,)), dma((SLOTS,)), dma((2,)), dma((2,)),
            dma((SLOTS,)), dma((SLOTS,)), dma((groups,)), dma((groups,)),
        ],
        compiler_params=pltpu.CompilerParams(
            collective_id=0, has_side_effects=True, vmem_limit_bytes=40 * 1024 * 1024
        ),
        name="couple",
    )(
        *(
            pltpu.with_memory_space_constraint(x, pltpu.HBM)
            for x in (
                deflation.reshape(K * layers, width), conductivity[0], storage[0],
                interface_rows[0, 0], interface_counts,
            )
        )
    )


def solution(mesh):
    placed = (
        P("sub", None, "coarse", None),
        P("sub", "coarse", None),
        P("sub", "coarse", None),
        P("sub", "coarse", None, None),
        P("sub", "coarse", None),
    )
    return jax.shard_map(
        functools.partial(body, mesh.shape["sub"], mesh.shape["coarse"]),
        mesh=mesh,
        in_specs=placed,
        out_specs=(P("sub", None, None), P("sub", "coarse", None, None)),
        check_vma=False,
    )
```
